256 devices in a mesh: dp: 32 (over y_lo, z, core), tp: 8 (over x, y_hi).
Axes of the slice: x: 4, y: 4 (y_hi: 2, y_lo: 2; y = y_hi * 2 + y_lo), z: 8, core: 2. Of those that a mesh axis runs over, the one named last changes fastest.
Arguments:
- inputs: bfloat16 [1024, 8192], P(('dp', 'tp')), may hold values from -6 to 6
- out_grad: bfloat16 [1024, 8192], P(('dp', 'tp')), may hold values from -6 to 6
- gate_weight: bfloat16 [8192, 15360], P('dp', 'tp'), may hold values from -0.0625 to 0.0625
- up_weight: bfloat16 [8192, 15360], P('dp', 'tp'), may hold values from -0.0625 to 0.0625
- down_weight: bfloat16 [15360, 8192], P('tp', 'dp'), may hold values from -0.046875 to 0.046875
Outputs:
- grad_inputs: float32 [1024, 8192], P(('dp', 'tp'))
- grad_gate: float32 [8192, 15360], P('dp', 'tp')
- grad_up: float32 [8192, 15360], P('dp', 'tp')
- grad_down: float32 [15360, 8192], P('tp', 'dp')
The draws below stay inside these ranges and needn't reach their ends.
All inputs are finite; a program needn't handle non-finite values.
Results may differ from the reference program's by a relative error of at most 0.0029.
Values may be sent and summed in bfloat16 or wider, within the bound.
A program may use at most 128 MiB of HBM per device.

```python
import jax
import jax.numpy as jnp

D = 8192
FF = 15360
TOKENS = 1024


def block_levels(own_key, extent, cuts, low, largest):
    loudness, own = 1.0, jax.random.fold_in(own_key, 6)
    for dim, blocks in cuts:
        draws = jnp.exp(jax.random.uniform(jax.random.fold_in(own, dim), (blocks,), jnp.float32, low / len(cuts), largest / len(cuts)))
        loudness = loudness * jnp.repeat(draws, extent[dim] // blocks).reshape([-1 if axis == dim else 1 for axis in range(len(extent))])
    return loudness


def bell_draw(own_key, extent, width, reach, cuts=(), dtype=jnp.bfloat16):
    factor_of = block_levels(own_key, extent, cuts, -0.22, 0.18) if cuts else 1.0
    values = jax.random.normal(own_key, extent, jnp.float32) * width * factor_of
    return jnp.minimum(jnp.maximum(values, -reach), reach).astype(dtype)


def setup_inputs(seed: int = 0) -> dict:
    key_of = jax.random.split(jax.random.key(seed), 6)
    inputs = bell_draw(key_of[0], (TOKENS, D), 1.0, 6.0, ((0, 256),))
    out_grad = bell_draw(key_of[1], (TOKENS, D), 1.0, 6.0, ((0, 256),))
    gate_weight = bell_draw(key_of[2], (D, FF), D ** -0.5, 0.0625, ((0, 32), (1, 8)))
    up_weight = bell_draw(key_of[3], (D, FF), D ** -0.5, 0.0625, ((0, 32), (1, 8)))
    down_weight = bell_draw(key_of[4], (FF, D), FF ** -0.5, 0.046875, ((0, 8), (1, 32)))
    return dict(inputs=inputs, out_grad=out_grad, gate_weight=gate_weight, up_weight=up_weight, down_weight=down_weight)


def swiglu_back(gate, up_proj, back_hidden):
    sigmoid_gate = jax.nn.sigmoid(gate)
    activated = gate * sigmoid_gate
    hidden = (activated * up_proj).astype(jnp.bfloat16)
    grad_up_act = (back_hidden * activated).astype(jnp.bfloat16)
    grad_gate_act = (back_hidden * up_proj * sigmoid_gate * (1.0 + gate * (1.0 - sigmoid_gate))).astype(jnp.bfloat16)
    return hidden, grad_gate_act, grad_up_act


def reference(inputs, out_grad, gate_weight, up_weight, down_weight):
    gate = jnp.dot(inputs, gate_weight, preferred_element_type=jnp.float32)
    up_proj = jnp.dot(inputs, up_weight, preferred_element_type=jnp.float32)
    back_hidden = jnp.dot(out_grad, down_weight.T, preferred_element_type=jnp.float32)
    hidden, grad_gate_act, grad_up_act = swiglu_back(gate, up_proj, back_hidden)
    grad_inputs = (jnp.dot(grad_gate_act, gate_weight.T, preferred_element_type=jnp.float32)
                   + jnp.dot(grad_up_act, up_weight.T, preferred_element_type=jnp.float32))
    grad_gate = jnp.dot(inputs.T, grad_gate_act, preferred_element_type=jnp.float32)
    grad_up = jnp.dot(inputs.T, grad_up_act, preferred_element_type=jnp.float32)
    grad_down = jnp.dot(hidden.T, out_grad, preferred_element_type=jnp.float32)
    return grad_inputs, grad_gate, grad_up, grad_down
```

```python
import jax
import jax.numpy as jnp
from jax import lax
from jax.experimental import pallas as pl
from jax.experimental.pallas import tpu as pltpu
from jax.sharding import PartitionSpec as P

MESH = pl.DeviceIdType.MESH
F32, BF16 = jnp.float32, jnp.bfloat16
NZ, NYZ, NTP = 8, 16, 8
OWN = 4
DC = 256
FF = 1920
CA = 896
HA = 512
HB = 512
UP, DOWN = 0, 1
TILES = ((0, 512), (512, 384), (896, 512), (1408, 512))


SCALE = 2.0**19
TINY = 2.0**-126


def coded(v):
    return (v * jnp.abs(v) * (v * v)).astype(BF16)


def decoded(y):
    y = y.astype(F32)
    r = lax.rsqrt(jnp.maximum(jnp.abs(y), TINY))
    return y * r * r * lax.rsqrt(r)


def dot(a, b):
    return jnp.dot(a, b, preferred_element_type=F32)


def dot_nt(a, b):
    return lax.dot_general(a, b, (((1,), (1,)), ((), ())), preferred_element_type=F32)


def kernel(
    x_ref, g_ref, wg_ref, wu_ref, wd_ref,
    gi_ref, og_ref, ou_ref, od_ref,
    stage, first, tokens, xs, xts, xtp, wgs, wus, wds, part,
    ya_s, ya_r, zb_s, zb_r, za_s, za_r, yb_s, yb_r, acts,
    gi, gi_r, fin_s, fin_r, odt,
    first_ss, first_rs, tok_ss, tok_rs, w_ls, w_ss, w_rs, xt_ss, xt_rs,
    ya_ss, ya_rs, zb_ss, zb_rs, za_ss, za_rs, yb_ss, yb_rs,
    aza_ss, aza_rs, azb_ss, azb_rs, aya_ss, aya_rs, ayb_ss, ayb_rs, core_ss, core_rs,
    gi_ss, gi_rs, fin_ss, fin_rs, out_ls,
):
    dp, tp = lax.axis_index("dp"), lax.axis_index("tp")
    c = lax.rem(dp, 2)
    yz = lax.div(dp, 2)
    z = lax.rem(yz, NZ)
    a = lax.div(yz, NZ)

    def at(yz_to):
        return (yz_to * 2 + c, tp)

    def at_z(step):
        return at(a * NZ + lax.rem(z + step + NZ, NZ))

    other_y = at((1 - a) * NZ + z)
    other_core = (yz * 2 + 1 - c, tp)
    z_next = (at_z(1), at_z(-1))

    def yz_off(k):
        return lax.rem(yz + k + NYZ, NYZ)

    def tp_off(k):
        return lax.rem(tp + k + NTP, NTP)

    def remote(src, dst, ss, rs, to):
        return pltpu.make_async_remote_copy(
            src_ref=src, dst_ref=dst, send_sem=ss, recv_sem=rs, device_id=to, device_id_type=MESH
        )

    def z_rows(step):
        return pl.ds(pl.multiple_of(lax.rem(z + step + NZ, NZ) * 32, 32), 32)

    barrier = pltpu.get_barrier_semaphore()
    for k in range(1, NYZ):
        pl.semaphore_signal(barrier, inc=1, device_id=at(yz_off(k)), device_id_type=MESH)
    for k in range(1, NTP):
        pl.semaphore_signal(barrier, inc=1, device_id=(dp, tp_off(k)), device_id_type=MESH)
    pl.semaphore_signal(barrier, inc=1, device_id=other_core, device_id_type=MESH)

    w_local = []
    mine = pl.ds(pl.multiple_of(c * DC, DC), DC)
    slots = (wgs.at[mine], wus.at[mine], wds.at[c])
    for i, (src, dst) in enumerate(zip((wg_ref, wu_ref, wd_ref), slots)):
        copy = pltpu.make_async_copy(src, dst, w_ls.at[i])
        copy.start()
        w_local.append(copy)

    for n, ref in enumerate((x_ref, g_ref)):
        whole = ref[...].astype(F32)
        for i in range(64):
            stage[i * 4 : i * 4 + 4, :] = whole[:, i * 128 : i * 128 + 128]
        first[n] = stage[0:256, :].astype(BF16).reshape(NYZ, 16, 128)

    pl.semaphore_wait(barrier, NYZ - 1 + NTP - 1 + 1)

    sends = []
    for k in range(1, NYZ):
        copy = remote(
            first.at[:, yz_off(k)], tokens.at[:, tp, yz], first_ss.at[k], first_rs.at[k], at(yz_off(k))
        )
        copy.start()
        sends.append(copy)
    for i, (src, dst) in enumerate(zip((wg_ref, wu_ref, wd_ref), slots)):
        copy = remote(src, dst, w_ss.at[i], w_rs.at[i], other_core)
        copy.start()
        sends.append(copy)
    tokens[:, tp, yz] = first[:, yz]
    for k in range(1, NYZ):
        piece = tokens.at[:, tp, yz_off(-k)]
        remote(piece, piece, first_ss.at[k], first_rs.at[k], at(yz_off(-k))).wait_recv()
    for n in range(2):
        for k in range(1, NTP):
            copy = remote(
                tokens.at[n, tp], tokens.at[n, tp], tok_ss.at[n, k], tok_rs.at[n, k], (dp, tp_off(k))
            )
            copy.start()
            sends.append(copy)

    def take_tokens(n):
        for k in range(1, NTP):
            piece = tokens.at[n, tp_off(-k)]
            remote(piece, piece, tok_ss.at[n, k], tok_rs.at[n, k], (dp, tp_off(-k))).wait_recv()
        stage[...] = tokens[n].reshape(NTP * NYZ * 16, 128).astype(F32)
        for d in range(4):
            for t in range(OWN):
                block = stage[pl.ds(d * 4 + t, 128, stride=16), :]
                rows, cols = slice(t * 128, t * 128 + 128), slice(d % 2 * 128, d % 2 * 128 + 128)
                xs[n, d // 2, rows, cols] = block.astype(BF16)
                xts[n, d // 2, cols, rows] = block.T.astype(BF16)
        copy = remote(xts.at[n, 1 - c], xtp.at[n], xt_ss.at[n], xt_rs.at[n], other_core)
        copy.start()
        sends.append(copy)

    def take_weight(i):
        w_local[i].wait()
        theirs = (
            wgs.at[pl.ds(pl.multiple_of((1 - c) * DC, DC), DC)],
            wus.at[pl.ds(pl.multiple_of((1 - c) * DC, DC), DC)],
            wds.at[1 - c],
        )[i]
        remote(theirs, theirs, w_ss.at[i], w_rs.at[i], other_core).wait_recv()

    def b_cols(direction, s):
        if s == 0:
            return (CA, CA + HB) if direction == UP else (CA + HB, FF)
        return (CA, FF)

    def a_cols(direction, s):
        if s == 0:
            return (0, HA) if direction == UP else (HA, CA)
        return (0, CA)

    def first_products(t):
        if t < 2:
            w = (wgs, wus)[t]
            for lo, size in TILES:
                cols = slice(lo, lo + size)
                value = dot(xs[0, 0], w[0:DC, cols]) + dot(xs[0, 1], w[DC : 2 * DC, cols])
                part[t, :, :, cols] = (value * SCALE).reshape(2, 256, size)
        else:
            for lo, size in TILES:
                cols = slice(lo, lo + size)
                value = dot_nt(xs[1, 0], wds[0, cols, :]) + dot_nt(xs[1, 1], wds[1, cols, :])
                part[t, :, :, cols] = (value * SCALE).reshape(2, 256, size)
        ya_s[t] = coded(part[t, 1 - a, :, 0:CA])
        copy = remote(ya_s.at[t], ya_r.at[t], ya_ss.at[t], ya_rs.at[t], other_y)
        copy.start()
        sends.append(copy)

    def b_message(buf, direction, s, t):
        lo, hi = b_cols(direction, s)
        return buf.at[direction, s, t, :, :, pl.ds(lo - CA, hi - lo)]

    def a_message(buf, direction, s, t):
        lo, hi = a_cols(direction, s)
        return buf.at[direction, s, t, :, pl.ds(lo, hi - lo)]

    def b_wait(direction, s, t):
        got = b_message(zb_r, direction, s, t)
        remote(got, got, zb_ss.at[direction, s, t], zb_rs.at[direction, s, t], z_next[direction]).wait_recv()

    def a_wait(direction, s, t):
        got = a_message(za_r, direction, s, t)
        remote(got, got, za_ss.at[direction, s, t], za_rs.at[direction, s, t], z_next[direction]).wait_recv()

    def b_step(s, t):
        for direction in (UP, DOWN):
            rows = z_rows(4 - s if direction == UP else s - 4)
            lo, hi = b_cols(direction, s)
            if s == 0:
                zb_s[direction, s, t, :, :, lo - CA : hi - CA] = coded(part[t, :, rows, lo:hi])
            else:
                b_wait(direction, s - 1, t)
                glo, ghi = b_cols(direction, s - 1)
                zb_s[direction, s, t, :, :, glo - CA : ghi - CA] = coded(
                    part[t, :, rows, glo:ghi]
                    + decoded(zb_r[direction, s - 1, t, :, :, glo - CA : ghi - CA])
                )
                if s == 1:
                    nlo, nhi = b_cols(1 - direction, 0)
                    zb_s[direction, s, t, :, :, nlo - CA : nhi - CA] = coded(part[t, :, rows, nlo:nhi])
            copy = remote(
                b_message(zb_s, direction, s, t), b_message(zb_r, direction, s, t),
                zb_ss.at[direction, s, t], zb_rs.at[direction, s, t], z_next[direction],
            )
            copy.start()
            sends.append(copy)

    def b_end(t):
        own = z_rows(0)
        for direction in (UP, DOWN):
            b_wait(direction, 3, t)
        total = part[t, :, own, CA:FF] + decoded(zb_r[UP, 3, t]) + decoded(zb_r[DOWN, 3, t])
        part[t, :, own, CA:FF] = total
        yb_s[t] = coded(part[t, 1 - a, own, CA:FF])
        copy = remote(yb_s.at[t], yb_r.at[t], yb_ss.at[t], yb_rs.at[t], other_y)
        copy.start()
        sends.append(copy)

    def a_start(t):
        remote(ya_r.at[t], ya_r.at[t], ya_ss.at[t], ya_rs.at[t], other_y).wait_recv()
        part[t, a, :, 0:CA] = part[t, a, :, 0:CA] + decoded(ya_r[t])
        a_step(0, t)

    def a_step(s, t):
        for direction in (UP, DOWN):
            rows = z_rows(4 - s if direction == UP else s - 4)
            lo, hi = a_cols(direction, s)
            if s == 0:
                za_s[direction, s, t, :, lo:hi] = coded(part[t, a, rows, lo:hi])
            else:
                a_wait(direction, s - 1, t)
                glo, ghi = a_cols(direction, s - 1)
                za_s[direction, s, t, :, glo:ghi] = coded(
                    part[t, a, rows, glo:ghi] + decoded(za_r[direction, s - 1, t, :, glo:ghi])
                )
                if s == 1:
                    nlo, nhi = a_cols(1 - direction, 0)
                    za_s[direction, s, t, :, nlo:nhi] = coded(part[t, a, rows, nlo:nhi])
            copy = remote(
                a_message(za_s, direction, s, t), a_message(za_r, direction, s, t),
                za_ss.at[direction, s, t], za_rs.at[direction, s, t], z_next[direction],
            )
            copy.start()
            sends.append(copy)

    take_tokens(0)
    take_weight(0)
    first_products(0)
    b_step(0, 0)
    take_weight(1)
    first_products(1)
    b_step(0, 1)
    take_tokens(1)
    take_weight(2)
    first_products(2)
    b_step(0, 2)
    for t in range(3):
        b_step(1, t)
    a_start(0)
    for t in range(3):
        b_step(2, t)
    a_start(1)
    a_step(1, 0)
    for t in range(3):
        b_step(3, t)
    a_start(2)
    a_step(1, 1)
    a_step(2, 0)
    for t in range(3):
        b_end(t)
    a_step(1, 2)
    a_step(2, 1)
    a_step(3, 0)
    a_step(2, 2)
    a_step(3, 1)
    a_step(3, 2)

    own = z_rows(0)
    for t in range(3):
        for direction in (UP, DOWN):
            a_wait(direction, 3, t)
        remote(yb_r.at[t], yb_r.at[t], yb_ss.at[t], yb_rs.at[t], other_y).wait_recv()

    def total(t, lo, hi):
        if hi <= CA:
            value = (
                part[t, a, own, lo:hi]
                + decoded(za_r[UP, 3, t, :, lo:hi])
                + decoded(za_r[DOWN, 3, t, :, lo:hi])
            )
        else:
            value = part[t, a, own, lo:hi] + decoded(yb_r[t, :, lo - CA : hi - CA])
        return value * (1.0 / SCALE)

    for lo, size in TILES:
        hi = lo + size
        gate, up, back = total(0, lo, hi), total(1, lo, hi), total(2, lo, hi)
        s = jax.nn.sigmoid(gate)
        silu = gate * s
        acts[0, c, a, own, lo:hi] = (back * up * s * (1.0 + gate * (1.0 - s))).astype(BF16)
        acts[1, c, a, own, lo:hi] = (back * silu).astype(BF16)
        acts[2, c, a, own, lo:hi] = (silu * up).astype(BF16)

    def hand_on(region, ss, rs, to):
        copy = remote(region, region, ss, rs, to)
        copy.start()
        return copy

    def piece_a(t, side, step, lo=0, hi=CA):
        return acts.at[t, c, side, z_rows(step), pl.ds(lo, hi - lo)]

    def piece_b(t, step, lo=CA, hi=FF):
        return acts.at[t, c, :, z_rows(step), pl.ds(lo, hi - lo)]

    def a_part(direction, s):
        return (0, CA) if s < 3 else ((0, HA) if direction == UP else (HA, CA))

    def b_part(direction, s):
        return (CA, FF) if s < 3 else ((CA, CA + HB) if direction == UP else (CA + HB, FF))

    for t in range(3):
        sends.append(
            hand_on(acts.at[t, c, a, own, pl.ds(CA, FF - CA)], ayb_ss.at[t], ayb_rs.at[t], other_y)
        )
        for direction in (UP, DOWN):
            sends.append(
                hand_on(piece_a(t, a, 0), aza_ss.at[direction, 0, t], aza_rs.at[direction, 0, t], z_next[direction])
            )
        hand_on(piece_a(t, a, 0), aya_ss.at[t], aya_rs.at[t], other_y)
        hand_on(acts.at[t, c, a, own], core_ss.at[t], core_rs.at[t], other_core)
    for t in range(3):
        theirs = acts.at[t, c, 1 - a, own, pl.ds(CA, FF - CA)]
        remote(theirs, theirs, ayb_ss.at[t], ayb_rs.at[t], other_y).wait_recv()
        for direction in (UP, DOWN):
            sends.append(
                hand_on(piece_b(t, 0), azb_ss.at[direction, 0, t], azb_rs.at[direction, 0, t], z_next[direction])
            )
        hand_on(theirs, core_ss.at[t], core_rs.at[t], other_core)

    def gather_a(s, t):
        for direction in (UP, DOWN):
            step = -1 - s if direction == UP else 1 + s
            got = piece_a(t, a, step, *a_part(direction, s))
            remote(
                got, got, aza_ss.at[direction, s, t], aza_rs.at[direction, s, t], z_next[direction]
            ).wait_recv()
            if s < 3:
                sends.append(
                    hand_on(
                        piece_a(t, a, step, *a_part(direction, s + 1)),
                        aza_ss.at[direction, s + 1, t], aza_rs.at[direction, s + 1, t], z_next[direction],
                    )
                )
            hand_on(got, aya_ss.at[t], aya_rs.at[t], other_y)
            hand_on(got, core_ss.at[t], core_rs.at[t], other_core)

    def gather_b(s, t):
        for direction in (UP, DOWN):
            step = -1 - s if direction == UP else 1 + s
            got = piece_b(t, step, *b_part(direction, s))
            remote(
                got, got, azb_ss.at[direction, s, t], azb_rs.at[direction, s, t], z_next[direction]
            ).wait_recv()
            if s < 3:
                sends.append(
                    hand_on(
                        piece_b(t, step, *b_part(direction, s + 1)),
                        azb_ss.at[direction, s + 1, t], azb_rs.at[direction, s + 1, t], z_next[direction],
                    )
                )
            hand_on(got, core_ss.at[t], core_rs.at[t], other_core)

    def gather_a_end(t):
        got = acts.at[t, c, 1 - a, :, pl.ds(0, CA)]
        remote(got, got, aya_ss.at[t], aya_rs.at[t], other_y).wait_recv()
        hand_on(got, core_ss.at[t], core_rs.at[t], other_core)

    for s in range(4):
        for t in range(3):
            gather_a(s, t)
        for t in range(3):
            gather_b(s, t)
    for t in range(3):
        gather_a_end(t)

    for t in range(OWN):
        side, rows = t // 2, slice(t % 2 * 128, t % 2 * 128 + 128)
        value = dot_nt(acts[0, c, side, rows, :], wgs[...]) + dot_nt(acts[1, c, side, rows, :], wus[...])
        gi[t] = value
    for k in range(1, NTP):
        theirs = pl.ds(pl.multiple_of(tp_off(k) * 16, 16), 16)
        copy = remote(gi.at[:, theirs], gi_r.at[tp], gi_ss.at[k], gi_rs.at[k], (dp, tp_off(k)))
        copy.start()
        sends.append(copy)

    for n in range(2):
        remote(xtp.at[n], xtp.at[n], xt_ss.at[n], xt_rs.at[n], other_core).wait_recv()

    outs = []

    def weight_gradient(t, n):
        got = acts.at[t, 1 - c]
        remote(got, got, core_ss.at[t], core_rs.at[t], other_core).wait_recv()
        for lo, size in TILES:
            cols = slice(lo, lo + size)
            value = dot(xts[n, c], acts[t, c, :, :, cols].reshape(512, size)) + dot(
                xtp[n], acts[t, 1 - c, :, :, cols].reshape(512, size)
            )
            if t < 2:
                part[t, 0, :, cols] = value
            else:
                odt[cols, :] = value.T
        src, dst = ((part.at[0, 0], og_ref), (part.at[1, 0], ou_ref), (odt, od_ref))[t]
        copy = pltpu.make_async_copy(src, dst, out_ls.at[t])
        copy.start()
        outs.append(copy)

    weight_gradient(0, 0)

    mine16 = pl.ds(pl.multiple_of(tp * 16, 16), 16)
    for k in range(1, NTP):
        got = gi_r.at[tp_off(-k)]
        remote(got, got, gi_ss.at[k], gi_rs.at[k], (dp, tp_off(-k))).wait_recv()
    gi_r[tp] = jnp.zeros((OWN, 16, 512), F32)
    for t in range(OWN):
        value = gi[t, mine16, :]
        for k in range(NTP):
            value += gi_r[k, t]
        for d in range(4):
            fin_s[pl.ds(d * 4 + t, NYZ, stride=16), :] = value[:, d * 128 : d * 128 + 128]
    for k in range(1, NYZ):
        theirs = pl.ds(pl.multiple_of(yz_off(k) * 16, 16), 16)
        copy = remote(fin_s.at[theirs], fin_r.at[yz], fin_ss.at[k], fin_rs.at[k], at(yz_off(k)))
        copy.start()
        sends.append(copy)
    fin_r[yz] = fin_s[pl.ds(pl.multiple_of(yz * 16, 16), 16), :]

    weight_gradient(1, 0)
    weight_gradient(2, 1)

    for k in range(1, NYZ):
        got = fin_r.at[yz_off(-k)]
        remote(got, got, fin_ss.at[k], fin_rs.at[k], at(yz_off(-k))).wait_recv()
    for j in range(NYZ):
        for d in range(4):
            gi_ref[:, j * 512 + d * 128 : j * 512 + d * 128 + 128] = fin_r[j, d * 4 : d * 4 + 4, :]

    for copy in sends:
        copy.wait_send()
    for t in range(3):
        sent = acts.at[t, c, a, :, pl.ds(0, CA)]
        remote(sent, sent, aya_ss.at[t], aya_rs.at[t], other_y).wait_send()
        sent = acts.at[t, c]
        remote(sent, sent, core_ss.at[t], core_rs.at[t], other_core).wait_send()
    for copy in outs:
        copy.wait()


def per_device(inputs, out_grad, gate_weight, up_weight, down_weight):
    vmem = pl.BlockSpec(memory_space=pltpu.VMEM)
    hbm = pl.BlockSpec(memory_space=pl.ANY)
    dma = pltpu.SemaphoreType.DMA
    return pl.pallas_call(
        kernel,
        out_shape=(
            jax.ShapeDtypeStruct((OWN, 8192), F32),
            jax.ShapeDtypeStruct((DC, FF), F32),
            jax.ShapeDtypeStruct((DC, FF), F32),
            jax.ShapeDtypeStruct((FF, DC), F32),
        ),
        in_specs=[vmem, vmem, hbm, hbm, hbm],
        out_specs=(vmem, hbm, hbm, hbm),
        scratch_shapes=[
            pltpu.VMEM((NTP * NYZ * 16, 128), F32),
            pltpu.VMEM((2, NYZ, 16, 128), BF16),
            pltpu.VMEM((2, NTP, NYZ, 16, 128), BF16),
            pltpu.VMEM((2, 2, 512, DC), BF16),
            pltpu.VMEM((2, 2, DC, 512), BF16),
            pltpu.VMEM((2, DC, 512), BF16),
            pltpu.VMEM((2 * DC, FF), BF16),
            pltpu.VMEM((2 * DC, FF), BF16),
            pltpu.VMEM((2, FF, DC), BF16),
            pltpu.VMEM((3, 2, 256, FF), F32),
            pltpu.VMEM((3, 256, CA), BF16),
            pltpu.VMEM((3, 256, CA), BF16),
            pltpu.VMEM((2, 4, 3, 2, 32, FF - CA), BF16),
            pltpu.VMEM((2, 4, 3, 2, 32, FF - CA), BF16),
            pltpu.VMEM((2, 4, 3, 32, CA), BF16),
            pltpu.VMEM((2, 4, 3, 32, CA), BF16),
            pltpu.VMEM((3, 32, FF - CA), BF16),
            pltpu.VMEM((3, 32, FF - CA), BF16),
            pltpu.VMEM((3, 2, 2, 256, FF), BF16),
            pltpu.VMEM((OWN, 128, 512), F32),
            pltpu.VMEM((NTP, OWN, 16, 512), F32),
            pltpu.VMEM((NYZ * 16, 128), F32),
            pltpu.VMEM((NYZ, 16, 128), F32),
            pltpu.VMEM((FF, DC), F32),
            dma((NYZ,)), dma((NYZ,)), dma((2, NTP)), dma((2, NTP)),
            dma((3,)), dma((3,)), dma((3,)), dma((2,)), dma((2,)),
            dma((3,)), dma((3,)), dma((2, 4, 3)), dma((2, 4, 3)),
            dma((2, 4, 3)), dma((2, 4, 3)), dma((3,)), dma((3,)),
            dma((2, 4, 3)), dma((2, 4, 3)), dma((2, 4, 3)), dma((2, 4, 3)),
            dma((3,)), dma((3,)), dma((3,)), dma((3,)), dma((3,)), dma((3,)),
            dma((NTP,)), dma((NTP,)), dma((NYZ,)), dma((NYZ,)), dma((3,)),
        ],
        compiler_params=pltpu.CompilerParams(
            collective_id=0, has_side_effects=True, vmem_limit_bytes=60 * 1024 * 1024
        ),
    )(inputs, out_grad, gate_weight, up_weight, down_weight)


def solution(mesh):
    in_specs = (
        P(("dp", "tp"), None),
        P(("dp", "tp"), None),
        P("dp", "tp"),
        P("dp", "tp"),
        P("tp", "dp"),
    )
    out_specs = (P(("dp", "tp"), None), P("dp", "tp"), P("dp", "tp"), P("tp", "dp"))
    return jax.shard_map(
        per_device, mesh=mesh, in_specs=in_specs, out_specs=out_specs, check_vma=False
    )
```

```python
import jax
import jax.numpy as jnp
from jax import lax
from jax.experimental import pallas as pl
from jax.experimental.pallas import tpu as pltpu
from jax.sharding import PartitionSpec as P

MESH = pl.DeviceIdType.MESH
F32, BF16 = jnp.float32, jnp.bfloat16
NZ, NYZ, NTP = 8, 16, 8
OWN = 4
DC = 256
FF = 1920
CA = 896
HA = 512
HB = 512
UP, DOWN = 0, 1
TILES = ((0, 512), (512, 384), (896, 512), (1408, 512))


SCALE = 2.0**19
TINY = 2.0**-126


def coded(v):
    return (v * jnp.abs(v) * (v * v)).astype(BF16)


def decoded(y):
    y = y.astype(F32)
    r = lax.rsqrt(jnp.maximum(jnp.abs(y), TINY))
    return y * r * r * lax.rsqrt(r)


def squared(v):
    return (v * jnp.abs(v)).astype(BF16)


def rooted(y):
    y = y.astype(F32)
    return y * lax.rsqrt(jnp.maximum(jnp.abs(y), TINY))


def dot(a, b):
    return jnp.dot(a, b, preferred_element_type=F32)


def dot_nt(a, b):
    return lax.dot_general(a, b, (((1,), (1,)), ((), ())), preferred_element_type=F32)


def kernel(
    x_ref, g_ref, wg_ref, wu_ref, wd_ref,
    gi_ref, og_ref, ou_ref, od_ref,
    stage, first, tokens, xs, xts, xtp, wgs, wus, wds, part,
    ya_s, ya_r, zb_s, zb_r, za_s, za_r, yb_s, yb_r, acts,
    gi, gi_s, gi_r, fin_s, fin_r,
    first_ss, first_rs, tok_ss, tok_rs, w_ls, w_ss, w_rs, xt_ss, xt_rs,
    ya_ss, ya_rs, zb_ss, zb_rs, za_ss, za_rs, yb_ss, yb_rs,
    aza_ss, aza_rs, azb_ss, azb_rs, aya_ss, aya_rs, ayb_ss, ayb_rs, core_ss, core_rs,
    gi_ss, gi_rs, fin_ss, fin_rs,
):
    dp, tp = lax.axis_index("dp"), lax.axis_index("tp")
    c = lax.rem(dp, 2)
    yz = lax.div(dp, 2)
    z = lax.rem(yz, NZ)
    a = lax.div(yz, NZ)

    def at(yz_to):
        return (yz_to * 2 + c, tp)

    def at_z(step):
        return at(a * NZ + lax.rem(z + step + NZ, NZ))

    other_y = at((1 - a) * NZ + z)
    other_core = (yz * 2 + 1 - c, tp)
    z_next = (at_z(1), at_z(-1))

    def yz_off(k):
        return lax.rem(yz + k + NYZ, NYZ)

    def tp_off(k):
        return lax.rem(tp + k + NTP, NTP)

    def remote(src, dst, ss, rs, to):
        return pltpu.make_async_remote_copy(
            src_ref=src, dst_ref=dst, send_sem=ss, recv_sem=rs, device_id=to, device_id_type=MESH
        )

    def z_rows(step):
        return pl.ds(pl.multiple_of(lax.rem(z + step + NZ, NZ) * 32, 32), 32)

    barrier = pltpu.get_barrier_semaphore()
    for k in range(1, NYZ):
        pl.semaphore_signal(barrier, inc=1, device_id=at(yz_off(k)), device_id_type=MESH)
    for k in range(1, NTP):
        pl.semaphore_signal(barrier, inc=1, device_id=(dp, tp_off(k)), device_id_type=MESH)
    pl.semaphore_signal(barrier, inc=1, device_id=other_core, device_id_type=MESH)

    w_local = []
    mine = pl.ds(pl.multiple_of(c * DC, DC), DC)
    slots = (wgs.at[mine], wus.at[mine], wds.at[c])
    for i, (src, dst) in enumerate(zip((wg_ref, wu_ref, wd_ref), slots)):
        copy = pltpu.make_async_copy(src, dst, w_ls.at[i])
        copy.start()
        w_local.append(copy)

    for n, ref in enumerate((x_ref, g_ref)):
        whole = ref[...].astype(F32)
        for i in range(64):
            stage[i * 4 : i * 4 + 4, :] = whole[:, i * 128 : i * 128 + 128]
        first[n] = stage[0:256, :].astype(BF16).reshape(NYZ, 16, 128)

    pl.semaphore_wait(barrier, NYZ - 1 + NTP - 1 + 1)

    sends = []
    for k in range(1, NYZ):
        copy = remote(
            first.at[:, yz_off(k)], tokens.at[:, tp, yz], first_ss.at[k], first_rs.at[k], at(yz_off(k))
        )
        copy.start()
        sends.append(copy)
    for i, (src, dst) in enumerate(zip((wg_ref, wu_ref, wd_ref), slots)):
        copy = remote(src, dst, w_ss.at[i], w_rs.at[i], other_core)
        copy.start()
        sends.append(copy)
    tokens[:, tp, yz] = first[:, yz]
    for k in range(1, NYZ):
        piece = tokens.at[:, tp, yz_off(-k)]
        remote(piece, piece, first_ss.at[k], first_rs.at[k], at(yz_off(-k))).wait_recv()
    def tokens_start(n):
        for k in range(1, NTP):
            copy = remote(
                tokens.at[n, tp], tokens.at[n, tp], tok_ss.at[n, k], tok_rs.at[n, k], (dp, tp_off(k))
            )
            copy.start()
            sends.append(copy)

    def tokens_wait(n):
        for k in range(1, NTP):
            piece = tokens.at[n, tp_off(-k)]
            remote(piece, piece, tok_ss.at[n, k], tok_rs.at[n, k], (dp, tp_off(-k))).wait_recv()

    def tokens_end(n):
        stage[...] = tokens[n].reshape(NTP * NYZ * 16, 128).astype(F32)
        for d in range(4):
            for t in range(OWN):
                block = stage[pl.ds(d * 4 + t, 128, stride=16), :]
                rows, cols = slice(t * 128, t * 128 + 128), slice(d % 2 * 128, d % 2 * 128 + 128)
                xs[n, d // 2, rows, cols] = block.astype(BF16)

    def transpose_tokens(n):
        for h in range(2):
            xts[n, h] = xs[n, h].astype(F32).T.astype(BF16)
        copy = remote(xts.at[n, 1 - c], xtp.at[n], xt_ss.at[n], xt_rs.at[n], other_core)
        copy.start()
        sends.append(copy)

    def take_weight(i):
        w_local[i].wait()
        theirs = (
            wgs.at[pl.ds(pl.multiple_of((1 - c) * DC, DC), DC)],
            wus.at[pl.ds(pl.multiple_of((1 - c) * DC, DC), DC)],
            wds.at[1 - c],
        )[i]
        remote(theirs, theirs, w_ss.at[i], w_rs.at[i], other_core).wait_recv()

    def b_cols(direction, s):
        if s == 0:
            return (CA, CA + HB) if direction == UP else (CA + HB, FF)
        return (CA, FF)

    def a_cols(direction, s):
        if s == 0:
            return (0, HA) if direction == UP else (HA, CA)
        return (0, CA)

    def first_products(t):
        if t < 2:
            w = (wgs, wus)[t]
            for lo, size in TILES:
                cols = slice(lo, lo + size)
                value = dot(xs[0, 0], w[0:DC, cols]) + dot(xs[0, 1], w[DC : 2 * DC, cols])
                part[t, :, :, cols] = (value * SCALE).reshape(2, 256, size)
        else:
            for lo, size in TILES:
                cols = slice(lo, lo + size)
                value = dot_nt(xs[1, 0], wds[0, cols, :]) + dot_nt(xs[1, 1], wds[1, cols, :])
                part[t, :, :, cols] = (value * SCALE).reshape(2, 256, size)
        ya_s[t] = coded(part[t, 1 - a, :, 0:CA])
        copy = remote(ya_s.at[t], ya_r.at[t], ya_ss.at[t], ya_rs.at[t], other_y)
        copy.start()
        sends.append(copy)

    def b_message(buf, direction, s, t):
        lo, hi = b_cols(direction, s)
        return buf.at[direction, s, t, :, :, pl.ds(lo - CA, hi - lo)]

    def a_message(buf, direction, s, t):
        lo, hi = a_cols(direction, s)
        return buf.at[direction, s, t, :, pl.ds(lo, hi - lo)]

    def b_wait(direction, s, t):
        got = b_message(zb_r, direction, s, t)
        remote(got, got, zb_ss.at[direction, s, t], zb_rs.at[direction, s, t], z_next[direction]).wait_recv()

    def a_wait(direction, s, t):
        got = a_message(za_r, direction, s, t)
        remote(got, got, za_ss.at[direction, s, t], za_rs.at[direction, s, t], z_next[direction]).wait_recv()

    def b_step(s, t):
        for direction in (UP, DOWN):
            rows = z_rows(4 - s if direction == UP else s - 4)
            lo, hi = b_cols(direction, s)
            if s == 0:
                zb_s[direction, s, t, :, :, lo - CA : hi - CA] = coded(part[t, :, rows, lo:hi])
            else:
                b_wait(direction, s - 1, t)
                glo, ghi = b_cols(direction, s - 1)
                zb_s[direction, s, t, :, :, glo - CA : ghi - CA] = coded(
                    part[t, :, rows, glo:ghi]
                    + decoded(zb_r[direction, s - 1, t, :, :, glo - CA : ghi - CA])
                )
                if s == 1:
                    nlo, nhi = b_cols(1 - direction, 0)
                    zb_s[direction, s, t, :, :, nlo - CA : nhi - CA] = coded(part[t, :, rows, nlo:nhi])
            copy = remote(
                b_message(zb_s, direction, s, t), b_message(zb_r, direction, s, t),
                zb_ss.at[direction, s, t], zb_rs.at[direction, s, t], z_next[direction],
            )
            copy.start()
            sends.append(copy)

    def b_end(t):
        own = z_rows(0)
        for direction in (UP, DOWN):
            b_wait(direction, 3, t)
        total = part[t, :, own, CA:FF] + decoded(zb_r[UP, 3, t]) + decoded(zb_r[DOWN, 3, t])
        part[t, :, own, CA:FF] = total
        yb_s[t] = coded(part[t, 1 - a, own, CA:FF])
        copy = remote(yb_s.at[t], yb_r.at[t], yb_ss.at[t], yb_rs.at[t], other_y)
        copy.start()
        sends.append(copy)

    def a_start(t):
        remote(ya_r.at[t], ya_r.at[t], ya_ss.at[t], ya_rs.at[t], other_y).wait_recv()
        part[t, a, :, 0:CA] = part[t, a, :, 0:CA] + decoded(ya_r[t])
        a_step(0, t)

    def a_step(s, t):
        for direction in (UP, DOWN):
            rows = z_rows(4 - s if direction == UP else s - 4)
            lo, hi = a_cols(direction, s)
            if s == 0:
                za_s[direction, s, t, :, lo:hi] = coded(part[t, a, rows, lo:hi])
            else:
                a_wait(direction, s - 1, t)
                glo, ghi = a_cols(direction, s - 1)
                za_s[direction, s, t, :, glo:ghi] = coded(
                    part[t, a, rows, glo:ghi] + decoded(za_r[direction, s - 1, t, :, glo:ghi])
                )
                if s == 1:
                    nlo, nhi = a_cols(1 - direction, 0)
                    za_s[direction, s, t, :, nlo:nhi] = coded(part[t, a, rows, nlo:nhi])
            copy = remote(
                a_message(za_s, direction, s, t), a_message(za_r, direction, s, t),
                za_ss.at[direction, s, t], za_rs.at[direction, s, t], z_next[direction],
            )
            copy.start()
            sends.append(copy)

    tokens_start(0)
    tokens_wait(0)
    tokens_start(1)
    tokens_end(0)
    take_weight(0)
    first_products(0)
    b_step(0, 0)
    take_weight(1)
    first_products(1)
    b_step(0, 1)
    tokens_wait(1)
    tokens_end(1)
    take_weight(2)
    first_products(2)
    b_step(0, 2)
    transpose_tokens(0)
    transpose_tokens(1)
    for t in range(3):
        b_step(1, t)
    a_start(0)
    for t in range(3):
        b_step(2, t)
    a_start(1)
    a_step(1, 0)
    for t in range(3):
        b_step(3, t)
    a_start(2)
    a_step(1, 1)
    a_step(2, 0)
    for t in range(3):
        b_end(t)
    a_step(1, 2)
    a_step(2, 1)
    a_step(3, 0)
    a_step(2, 2)
    a_step(3, 1)
    a_step(3, 2)

    own = z_rows(0)
    for t in range(3):
        for direction in (UP, DOWN):
            a_wait(direction, 3, t)
        remote(yb_r.at[t], yb_r.at[t], yb_ss.at[t], yb_rs.at[t], other_y).wait_recv()

    def total(t, lo, hi):
        if hi <= CA:
            value = (
                part[t, a, own, lo:hi]
                + decoded(za_r[UP, 3, t, :, lo:hi])
                + decoded(za_r[DOWN, 3, t, :, lo:hi])
            )
        else:
            value = part[t, a, own, lo:hi] + decoded(yb_r[t, :, lo - CA : hi - CA])
        return value * (1.0 / SCALE)

    for lo, size in TILES:
        hi = lo + size
        gate, up, back = total(0, lo, hi), total(1, lo, hi), total(2, lo, hi)
        s = jax.nn.sigmoid(gate)
        silu = gate * s
        acts[0, c, a, own, lo:hi] = (back * up * s * (1.0 + gate * (1.0 - s))).astype(BF16)
        acts[1, c, a, own, lo:hi] = (back * silu).astype(BF16)
        acts[2, c, a, own, lo:hi] = (silu * up).astype(BF16)

    def hand_on(region, ss, rs, to):
        copy = remote(region, region, ss, rs, to)
        copy.start()
        return copy

    def piece_a(t, side, step, lo=0, hi=CA):
        return acts.at[t, c, side, z_rows(step), pl.ds(lo, hi - lo)]

    def piece_b(t, step, lo=CA, hi=FF):
        return acts.at[t, c, :, z_rows(step), pl.ds(lo, hi - lo)]

    def a_part(direction, s):
        return (0, CA) if s < 3 else ((0, HA) if direction == UP else (HA, CA))

    def b_part(direction, s):
        return (CA, FF) if s < 3 else ((CA, CA + HB) if direction == UP else (CA + HB, FF))

    def gather_start(t):
        sends.append(
            hand_on(acts.at[t, c, a, own, pl.ds(CA, FF - CA)], ayb_ss.at[t], ayb_rs.at[t], other_y)
        )
        for direction in (UP, DOWN):
            sends.append(
                hand_on(piece_a(t, a, 0), aza_ss.at[direction, 0, t], aza_rs.at[direction, 0, t], z_next[direction])
            )
        hand_on(piece_a(t, a, 0), aya_ss.at[t], aya_rs.at[t], other_y)
        hand_on(acts.at[t, c, a, own], core_ss.at[t], core_rs.at[t], other_core)

    def gather_start_b(t):
        theirs = acts.at[t, c, 1 - a, own, pl.ds(CA, FF - CA)]
        remote(theirs, theirs, ayb_ss.at[t], ayb_rs.at[t], other_y).wait_recv()
        for direction in (UP, DOWN):
            sends.append(
                hand_on(piece_b(t, 0), azb_ss.at[direction, 0, t], azb_rs.at[direction, 0, t], z_next[direction])
            )
        hand_on(theirs, core_ss.at[t], core_rs.at[t], other_core)

    def gather_a(s, t):
        for direction in (UP, DOWN):
            step = -1 - s if direction == UP else 1 + s
            got = piece_a(t, a, step, *a_part(direction, s))
            remote(
                got, got, aza_ss.at[direction, s, t], aza_rs.at[direction, s, t], z_next[direction]
            ).wait_recv()
            if s < 3:
                sends.append(
                    hand_on(
                        piece_a(t, a, step, *a_part(direction, s + 1)),
                        aza_ss.at[direction, s + 1, t], aza_rs.at[direction, s + 1, t], z_next[direction],
                    )
                )
            hand_on(got, aya_ss.at[t], aya_rs.at[t], other_y)
            hand_on(got, core_ss.at[t], core_rs.at[t], other_core)

    def gather_b(s, t):
        for direction in (UP, DOWN):
            step = -1 - s if direction == UP else 1 + s
            got = piece_b(t, step, *b_part(direction, s))
            remote(
                got, got, azb_ss.at[direction, s, t], azb_rs.at[direction, s, t], z_next[direction]
            ).wait_recv()
            if s < 3:
                sends.append(
                    hand_on(
                        piece_b(t, step, *b_part(direction, s + 1)),
                        azb_ss.at[direction, s + 1, t], azb_rs.at[direction, s + 1, t], z_next[direction],
                    )
                )
            hand_on(got, core_ss.at[t], core_rs.at[t], other_core)

    def gather_a_end(t):
        got = acts.at[t, c, 1 - a, :, pl.ds(0, CA)]
        remote(got, got, aya_ss.at[t], aya_rs.at[t], other_y).wait_recv()
        hand_on(got, core_ss.at[t], core_rs.at[t], other_core)

    def input_gradient(t):
        side, rows = t // 2, slice(t % 2 * 128, t % 2 * 128 + 128)
        value = dot_nt(acts[0, c, side, rows, :], wgs[...]) + dot_nt(acts[1, c, side, rows, :], wus[...])
        gi[t] = value
        gi_s[t] = squared(value)

    def input_gradient_send():
        for k in range(1, NTP):
            theirs = pl.ds(pl.multiple_of(tp_off(k) * 16, 16), 16)
            copy = remote(gi_s.at[:, theirs], gi_r.at[tp], gi_ss.at[k], gi_rs.at[k], (dp, tp_off(k)))
            copy.start()
            sends.append(copy)

    def input_gradient_sum():
        mine16 = pl.ds(pl.multiple_of(tp * 16, 16), 16)
        for k in range(1, NTP):
            got = gi_r.at[tp_off(-k)]
            remote(got, got, gi_ss.at[k], gi_rs.at[k], (dp, tp_off(-k))).wait_recv()
        gi_r[tp] = jnp.zeros((OWN, 16, 512), BF16)
        for t in range(OWN):
            value = gi[t, mine16, :]
            for k in range(NTP):
                value += rooted(gi_r[k, t])
            for d in range(4):
                fin_s[pl.ds(d * 4 + t, NYZ, stride=16), :] = value[:, d * 128 : d * 128 + 128]
        for k in range(1, NYZ):
            theirs = pl.ds(pl.multiple_of(yz_off(k) * 16, 16), 16)
            copy = remote(fin_s.at[theirs], fin_r.at[yz], fin_ss.at[k], fin_rs.at[k], at(yz_off(k)))
            copy.start()
            sends.append(copy)
        fin_r[yz] = fin_s[pl.ds(pl.multiple_of(yz * 16, 16), 16), :]

    def weight_gradient(t, n):
        got = acts.at[t, 1 - c]
        remote(got, got, core_ss.at[t], core_rs.at[t], other_core).wait_recv()
        for lo, size in TILES:
            cols = slice(lo, lo + size)
            value = dot(xts[n, c], acts[t, c, :, :, cols].reshape(512, size)) + dot(
                xtp[n], acts[t, 1 - c, :, :, cols].reshape(512, size)
            )
            if t < 2:
                (og_ref, ou_ref)[t][:, cols] = value
            else:
                od_ref[cols, :] = value.T

    for t in range(2):
        gather_start(t)
    for t in range(2):
        gather_start_b(t)
    for s in range(4):
        for t in range(2):
            gather_a(s, t)
        for t in range(2):
            gather_b(s, t)
        if s == 2:
            gather_start(2)
    gather_start_b(2)
    for t in range(2):
        gather_a_end(t)
    input_gradient(0)
    input_gradient(1)
    gather_a(0, 2)
    gather_b(0, 2)
    input_gradient(2)
    input_gradient(3)
    input_gradient_send()
    gather_a(1, 2)
    gather_b(1, 2)
    for n in range(2):
        remote(xtp.at[n], xtp.at[n], xt_ss.at[n], xt_rs.at[n], other_core).wait_recv()
    weight_gradient(0, 0)
    gather_a(2, 2)
    gather_b(2, 2)
    weight_gradient(1, 0)
    gather_a(3, 2)
    gather_b(3, 2)
    gather_a_end(2)
    input_gradient_sum()
    weight_gradient(2, 1)

    for k in range(1, NYZ):
        got = fin_r.at[yz_off(-k)]
        remote(got, got, fin_ss.at[k], fin_rs.at[k], at(yz_off(-k))).wait_recv()
    for j in range(NYZ):
        for d in range(4):
            gi_ref[:, j * 512 + d * 128 : j * 512 + d * 128 + 128] = fin_r[j, d * 4 : d * 4 + 4, :]

    for copy in sends:
        copy.wait_send()
    for t in range(3):
        sent = acts.at[t, c, a, :, pl.ds(0, CA)]
        remote(sent, sent, aya_ss.at[t], aya_rs.at[t], other_y).wait_send()
        sent = acts.at[t, c]
        remote(sent, sent, core_ss.at[t], core_rs.at[t], other_core).wait_send()


def per_device(inputs, out_grad, gate_weight, up_weight, down_weight):
    vmem = pl.BlockSpec(memory_space=pltpu.VMEM)
    hbm = pl.BlockSpec(memory_space=pl.ANY)
    dma = pltpu.SemaphoreType.DMA
    return pl.pallas_call(
        kernel,
        out_shape=(
            pltpu.VMEM((OWN, 8192), F32),
            pltpu.VMEM((DC, FF), F32),
            pltpu.VMEM((DC, FF), F32),
            pltpu.VMEM((FF, DC), F32),
        ),
        in_specs=[vmem, vmem, hbm, hbm, hbm],
        out_specs=(vmem, vmem, vmem, vmem),
        scratch_shapes=[
            pltpu.VMEM((NTP * NYZ * 16, 128), F32),
            pltpu.VMEM((2, NYZ, 16, 128), BF16),
            pltpu.VMEM((2, NTP, NYZ, 16, 128), BF16),
            pltpu.VMEM((2, 2, 512, DC), BF16),
            pltpu.VMEM((2, 2, DC, 512), BF16),
            pltpu.VMEM((2, DC, 512), BF16),
            pltpu.VMEM((2 * DC, FF), BF16),
            pltpu.VMEM((2 * DC, FF), BF16),
            pltpu.VMEM((2, FF, DC), BF16),
            pltpu.VMEM((3, 2, 256, FF), F32),
            pltpu.VMEM((3, 256, CA), BF16),
            pltpu.VMEM((3, 256, CA), BF16),
            pltpu.VMEM((2, 4, 3, 2, 32, FF - CA), BF16),
            pltpu.VMEM((2, 4, 3, 2, 32, FF - CA), BF16),
            pltpu.VMEM((2, 4, 3, 32, CA), BF16),
            pltpu.VMEM((2, 4, 3, 32, CA), BF16),
            pltpu.VMEM((3, 32, FF - CA), BF16),
            pltpu.VMEM((3, 32, FF - CA), BF16),
            pltpu.VMEM((3, 2, 2, 256, FF), BF16),
            pltpu.VMEM((OWN, 128, 512), F32),
            pltpu.VMEM((OWN, 128, 512), BF16),
            pltpu.VMEM((NTP, OWN, 16, 512), BF16),
            pltpu.VMEM((NYZ * 16, 128), F32),
            pltpu.VMEM((NYZ, 16, 128), F32),
            dma((NYZ,)), dma((NYZ,)), dma((2, NTP)), dma((2, NTP)),
            dma((3,)), dma((3,)), dma((3,)), dma((2,)), dma((2,)),
            dma((3,)), dma((3,)), dma((2, 4, 3)), dma((2, 4, 3)),
            dma((2, 4, 3)), dma((2, 4, 3)), dma((3,)), dma((3,)),
            dma((2, 4, 3)), dma((2, 4, 3)), dma((2, 4, 3)), dma((2, 4, 3)),
            dma((3,)), dma((3,)), dma((3,)), dma((3,)), dma((3,)), dma((3,)),
            dma((NTP,)), dma((NTP,)), dma((NYZ,)), dma((NYZ,)),
        ],
        compiler_params=pltpu.CompilerParams(
            collective_id=0, has_side_effects=True, vmem_limit_bytes=56 * 1024 * 1024
        ),
    )(inputs, out_grad, gate_weight, up_weight, down_weight)


def solution(mesh):
    in_specs = (
        P(("dp", "tp"), None),
        P(("dp", "tp"), None),
        P("dp", "tp"),
        P("dp", "tp"),
        P("tp", "dp"),
    )
    out_specs = (P(("dp", "tp"), None), P("dp", "tp"), P("dp", "tp"), P("tp", "dp"))
    return jax.shard_map(
        per_device, mesh=mesh, in_specs=in_specs, out_specs=out_specs, check_vma=False
    )
```

```python
import jax
import jax.numpy as jnp
from jax import lax
from jax.experimental import pallas as pl
from jax.experimental.pallas import tpu as pltpu
from jax.sharding import PartitionSpec as P

MESH = pl.DeviceIdType.MESH
F32, BF16 = jnp.float32, jnp.bfloat16
NZ, NYZ, NTP = 8, 16, 8
OWN = 4
DC = 256
FF = 1920
CA = 896
HA = 512
HB = 512
UP, DOWN = 0, 1
TILES = ((0, 512), (512, 384), (896, 512), (1408, 512))
FAR_FIRST = (4, 3, -3, 2, -2, 1, -1, 0)


SCALE = 2.0**19
TINY = 2.0**-126


def coded(v):
    return (v * jnp.abs(v) * (v * v)).astype(BF16)


def decoded(y):
    y = y.astype(F32)
    r = lax.rsqrt(jnp.maximum(jnp.abs(y), TINY))
    return y * r * r * lax.rsqrt(r)


def squared(v):
    return (v * jnp.abs(v)).astype(BF16)


def rooted(y):
    y = y.astype(F32)
    return y * lax.rsqrt(jnp.maximum(jnp.abs(y), TINY))


def dot(a, b):
    return jnp.dot(a, b, preferred_element_type=F32)


def dot_nt(a, b):
    return lax.dot_general(a, b, (((1,), (1,)), ((), ())), preferred_element_type=F32)


def kernel(
    x_ref, g_ref, wg_ref, wu_ref, wd_ref,
    gi_ref, og_ref, ou_ref, od_ref,
    stage, first, tokens, xs, xts, xtp, wgs, wus, wds, part,
    ya_s, ya_r, zb_s, zb_r, za_s, za_r, yb_s, yb_r, acts,
    gi, gi_s, gi_r, fin_s, fin_r,
    first_ss, first_rs, tok_ss, tok_rs, w_ls, w_ss, w_rs, xt_ss, xt_rs,
    ya_ss, ya_rs, zb_ss, zb_rs, za_ss, za_rs, yb_ss, yb_rs,
    aza_ss, aza_rs, azb_ss, azb_rs, aya_ss, aya_rs, ayb_ss, ayb_rs, core_ss, core_rs,
    gi_ss, gi_rs, fin_ss, fin_rs,
):
    dp, tp = lax.axis_index("dp"), lax.axis_index("tp")
    c = lax.rem(dp, 2)
    yz = lax.div(dp, 2)
    z = lax.rem(yz, NZ)
    a = lax.div(yz, NZ)

    def at(yz_to):
        return (yz_to * 2 + c, tp)

    def at_z(step):
        return at(a * NZ + lax.rem(z + step + NZ, NZ))

    other_y = at((1 - a) * NZ + z)
    other_core = (yz * 2 + 1 - c, tp)
    z_next = (at_z(1), at_z(-1))

    def yz_off(k):
        return lax.rem(yz + k + NYZ, NYZ)

    def tp_off(k):
        return lax.rem(tp + k + NTP, NTP)

    def remote(src, dst, ss, rs, to):
        return pltpu.make_async_remote_copy(
            src_ref=src, dst_ref=dst, send_sem=ss, recv_sem=rs, device_id=to, device_id_type=MESH
        )

    def z_rows(step):
        return pl.ds(pl.multiple_of(lax.rem(z + step + NZ, NZ) * 32, 32), 32)

    barrier = pltpu.get_barrier_semaphore()
    for k in range(1, NYZ):
        pl.semaphore_signal(barrier, inc=1, device_id=at(yz_off(k)), device_id_type=MESH)
    for k in range(1, NTP):
        pl.semaphore_signal(barrier, inc=1, device_id=(dp, tp_off(k)), device_id_type=MESH)
    pl.semaphore_signal(barrier, inc=1, device_id=other_core, device_id_type=MESH)

    w_local = []
    mine = pl.ds(pl.multiple_of(c * DC, DC), DC)
    slots = (wgs.at[mine], wus.at[mine], wds.at[c])
    for i, (src, dst) in enumerate(zip((wg_ref, wu_ref, wd_ref), slots)):
        copy = pltpu.make_async_copy(src, dst, w_ls.at[i])
        copy.start()
        w_local.append(copy)

    for n, ref in enumerate((x_ref, g_ref)):
        whole = ref[...].astype(F32)
        for i in range(64):
            stage[i * 4 : i * 4 + 4, :] = whole[:, i * 128 : i * 128 + 128]
        first[n] = stage[0:256, :].astype(BF16).reshape(NYZ, 16, 128)

    pl.semaphore_wait(barrier, NYZ - 1 + NTP - 1 + 1)

    sends = []
    for k in range(1, NYZ):
        copy = remote(
            first.at[:, yz_off(k)], tokens.at[:, tp, yz], first_ss.at[k], first_rs.at[k], at(yz_off(k))
        )
        copy.start()
        sends.append(copy)
    for i, (src, dst) in enumerate(zip((wg_ref, wu_ref, wd_ref), slots)):
        copy = remote(src, dst, w_ss.at[i], w_rs.at[i], other_core)
        copy.start()
        sends.append(copy)
    tokens[:, tp, yz] = first[:, yz]
    for k in range(1, NYZ):
        piece = tokens.at[:, tp, yz_off(-k)]
        remote(piece, piece, first_ss.at[k], first_rs.at[k], at(yz_off(-k))).wait_recv()
    def tokens_start(n):
        for k in range(1, NTP):
            copy = remote(
                tokens.at[n, tp], tokens.at[n, tp], tok_ss.at[n, k], tok_rs.at[n, k], (dp, tp_off(k))
            )
            copy.start()
            sends.append(copy)

    def tokens_wait(n):
        for k in range(1, NTP):
            piece = tokens.at[n, tp_off(-k)]
            remote(piece, piece, tok_ss.at[n, k], tok_rs.at[n, k], (dp, tp_off(-k))).wait_recv()

    def tokens_end(n):
        stage[...] = tokens[n].reshape(NTP * NYZ * 16, 128).astype(F32)
        for d in range(4):
            for t in range(OWN):
                block = stage[pl.ds(d * 4 + t, 128, stride=16), :]
                rows, cols = slice(t * 128, t * 128 + 128), slice(d % 2 * 128, d % 2 * 128 + 128)
                xs[n, d // 2, rows, cols] = block.astype(BF16)

    def transpose_tokens(n):
        for h in range(2):
            xts[n, h] = xs[n, h].astype(F32).T.astype(BF16)
        copy = remote(xts.at[n, 1 - c], xtp.at[n], xt_ss.at[n], xt_rs.at[n], other_core)
        copy.start()
        sends.append(copy)

    def take_weight(i):
        w_local[i].wait()
        theirs = (
            wgs.at[pl.ds(pl.multiple_of((1 - c) * DC, DC), DC)],
            wus.at[pl.ds(pl.multiple_of((1 - c) * DC, DC), DC)],
            wds.at[1 - c],
        )[i]
        remote(theirs, theirs, w_ss.at[i], w_rs.at[i], other_core).wait_recv()

    def b_cols(direction, s):
        if s == 0:
            return (CA, CA + HB) if direction == UP else (CA + HB, FF)
        return (CA, FF)

    def a_cols(direction, s):
        if s == 0:
            return (0, HA) if direction == UP else (HA, CA)
        return (0, CA)

    def first_products(t):
        if t < 2:
            w = (wgs, wus)[t]
            for lo, size in TILES:
                cols = slice(lo, lo + size)
                value = dot(xs[0, 0], w[0:DC, cols]) + dot(xs[0, 1], w[DC : 2 * DC, cols])
                part[t, :, :, cols] = (value * SCALE).reshape(2, 256, size)
        else:
            for lo, size in TILES:
                cols = slice(lo, lo + size)
                value = dot_nt(xs[1, 0], wds[0, cols, :]) + dot_nt(xs[1, 1], wds[1, cols, :])
                part[t, :, :, cols] = (value * SCALE).reshape(2, 256, size)

    def y_send(t):
        ya_s[t] = coded(part[t, 1 - a, :, 0:CA])
        for i, rows in enumerate(y_pieces(t)):
            copy = remote(ya_s.at[t, rows], ya_r.at[t, rows], ya_ss.at[t, i], ya_rs.at[t, i], other_y)
            copy.start()
            sends.append(copy)

    def y_pieces(t):
        return [slice(0, 256)] if t < 2 else [z_rows(step) for step in FAR_FIRST]

    def y_take(t, i):
        rows = y_pieces(t)[i]
        remote(ya_r.at[t, rows], ya_r.at[t, rows], ya_ss.at[t, i], ya_rs.at[t, i], other_y).wait_recv()
        part[t, a, rows, 0:CA] = part[t, a, rows, 0:CA] + decoded(ya_r[t, rows, :])

    def b_message(buf, direction, s, t):
        lo, hi = b_cols(direction, s)
        return buf.at[direction, s, t, :, :, pl.ds(lo - CA, hi - lo)]

    def a_message(buf, direction, s, t):
        lo, hi = a_cols(direction, s)
        return buf.at[direction, s, t, :, pl.ds(lo, hi - lo)]

    def b_wait(direction, s, t):
        got = b_message(zb_r, direction, s, t)
        remote(got, got, zb_ss.at[direction, s, t], zb_rs.at[direction, s, t], z_next[direction]).wait_recv()

    def a_wait(direction, s, t):
        got = a_message(za_r, direction, s, t)
        remote(got, got, za_ss.at[direction, s, t], za_rs.at[direction, s, t], z_next[direction]).wait_recv()

    def b_step(s, t):
        for direction in (UP, DOWN):
            rows = z_rows(4 - s if direction == UP else s - 4)
            lo, hi = b_cols(direction, s)
            if s == 0:
                zb_s[direction, s, t, :, :, lo - CA : hi - CA] = coded(part[t, :, rows, lo:hi])
            else:
                b_wait(direction, s - 1, t)
                glo, ghi = b_cols(direction, s - 1)
                zb_s[direction, s, t, :, :, glo - CA : ghi - CA] = coded(
                    part[t, :, rows, glo:ghi]
                    + decoded(zb_r[direction, s - 1, t, :, :, glo - CA : ghi - CA])
                )
                if s == 1:
                    nlo, nhi = b_cols(1 - direction, 0)
                    zb_s[direction, s, t, :, :, nlo - CA : nhi - CA] = coded(part[t, :, rows, nlo:nhi])
            copy = remote(
                b_message(zb_s, direction, s, t), b_message(zb_r, direction, s, t),
                zb_ss.at[direction, s, t], zb_rs.at[direction, s, t], z_next[direction],
            )
            copy.start()
            sends.append(copy)

    def b_end(t):
        own = z_rows(0)
        for direction in (UP, DOWN):
            b_wait(direction, 3, t)
        total = part[t, :, own, CA:FF] + decoded(zb_r[UP, 3, t]) + decoded(zb_r[DOWN, 3, t])
        part[t, :, own, CA:FF] = total
        yb_s[t] = coded(part[t, 1 - a, own, CA:FF])
        copy = remote(yb_s.at[t], yb_r.at[t], yb_ss.at[t], yb_rs.at[t], other_y)
        copy.start()
        sends.append(copy)

    def a_start(t):
        y_take(t, 0)
        a_step(0, t)

    def a_step(s, t):
        if t == 2 and s > 0:
            y_take(t, 2 * s - 1)
            y_take(t, 2 * s)
        for direction in (UP, DOWN):
            rows = z_rows(4 - s if direction == UP else s - 4)
            lo, hi = a_cols(direction, s)
            if s == 0:
                za_s[direction, s, t, :, lo:hi] = coded(part[t, a, rows, lo:hi])
            else:
                a_wait(direction, s - 1, t)
                glo, ghi = a_cols(direction, s - 1)
                za_s[direction, s, t, :, glo:ghi] = coded(
                    part[t, a, rows, glo:ghi] + decoded(za_r[direction, s - 1, t, :, glo:ghi])
                )
                if s == 1:
                    nlo, nhi = a_cols(1 - direction, 0)
                    za_s[direction, s, t, :, nlo:nhi] = coded(part[t, a, rows, nlo:nhi])
            copy = remote(
                a_message(za_s, direction, s, t), a_message(za_r, direction, s, t),
                za_ss.at[direction, s, t], za_rs.at[direction, s, t], z_next[direction],
            )
            copy.start()
            sends.append(copy)

    tokens_start(0)
    tokens_wait(0)
    tokens_start(1)
    tokens_end(0)
    take_weight(0)
    first_products(0)
    b_step(0, 0)
    y_send(0)
    take_weight(1)
    first_products(1)
    b_step(0, 1)
    y_send(1)
    b_step(1, 0)
    b_step(1, 1)
    tokens_wait(1)
    tokens_end(1)
    take_weight(2)
    first_products(2)
    b_step(0, 2)
    y_send(2)
    b_step(2, 0)
    b_step(2, 1)
    b_step(1, 2)
    transpose_tokens(0)
    transpose_tokens(1)
    a_start(0)
    b_step(3, 0)
    b_step(3, 1)
    b_step(2, 2)
    a_start(1)
    a_step(1, 0)
    b_end(0)
    b_end(1)
    b_step(3, 2)
    a_start(2)
    a_step(1, 1)
    a_step(2, 0)
    b_end(2)
    a_step(1, 2)
    a_step(2, 1)
    a_step(3, 0)
    a_step(2, 2)
    a_step(3, 1)
    a_step(3, 2)

    own = z_rows(0)
    y_take(2, 7)
    for t in range(3):
        for direction in (UP, DOWN):
            a_wait(direction, 3, t)
        remote(yb_r.at[t], yb_r.at[t], yb_ss.at[t], yb_rs.at[t], other_y).wait_recv()

    def total(t, lo, hi):
        if hi <= CA:
            value = (
                part[t, a, own, lo:hi]
                + decoded(za_r[UP, 3, t, :, lo:hi])
                + decoded(za_r[DOWN, 3, t, :, lo:hi])
            )
        else:
            value = part[t, a, own, lo:hi] + decoded(yb_r[t, :, lo - CA : hi - CA])
        return value * (1.0 / SCALE)

    for lo, size in TILES:
        hi = lo + size
        gate, up, back = total(0, lo, hi), total(1, lo, hi), total(2, lo, hi)
        s = jax.nn.sigmoid(gate)
        silu = gate * s
        acts[0, c, a, own, lo:hi] = (back * up * s * (1.0 + gate * (1.0 - s))).astype(BF16)
        acts[1, c, a, own, lo:hi] = (back * silu).astype(BF16)
        acts[2, c, a, own, lo:hi] = (silu * up).astype(BF16)

    def hand_on(region, ss, rs, to):
        copy = remote(region, region, ss, rs, to)
        copy.start()
        return copy

    def piece_a(t, side, step, lo=0, hi=CA):
        return acts.at[t, c, side, z_rows(step), pl.ds(lo, hi - lo)]


    def a_part(direction, s):
        return (0, CA) if s < 3 else ((0, HA) if direction == UP else (HA, CA))

    def b_part(direction, s):
        return (CA, FF) if s < 3 else ((CA, CA + HB) if direction == UP else (CA + HB, FF))

    def gather_start(t):
        sends.append(
            hand_on(acts.at[t, c, a, own, pl.ds(CA, FF - CA)], ayb_ss.at[t], ayb_rs.at[t], other_y)
        )
        for direction in (UP, DOWN):
            sends.append(
                hand_on(piece_a(t, a, 0), aza_ss.at[direction, 0, t], aza_rs.at[direction, 0, t], z_next[direction])
            )
        hand_on(piece_a(t, a, 0), aya_ss.at[t], aya_rs.at[t], other_y)
        hand_on(acts.at[t, c, a, own], core_ss.at[t], core_rs.at[t], other_core)
        for direction in (UP, DOWN):
            b_hand_on(0, direction, 0, t, 0, CA, FF)

    def b_hand_on(chain, direction, s, t, step, lo, hi):
        sends.append(
            hand_on(
                piece_a(t, a if chain == 0 else 1 - a, step, lo, hi),
                azb_ss.at[chain, direction, s, t], azb_rs.at[chain, direction, s, t], z_next[direction],
            )
        )

    def gather_start_b(t):
        theirs = acts.at[t, c, 1 - a, own, pl.ds(CA, FF - CA)]
        remote(theirs, theirs, ayb_ss.at[t], ayb_rs.at[t], other_y).wait_recv()
        for direction in (UP, DOWN):
            b_hand_on(1, direction, 0, t, 0, CA, FF)
        hand_on(theirs, core_ss.at[t], core_rs.at[t], other_core)

    def gather_a(s, t):
        for direction in (UP, DOWN):
            step = -1 - s if direction == UP else 1 + s
            got = piece_a(t, a, step, *a_part(direction, s))
            remote(
                got, got, aza_ss.at[direction, s, t], aza_rs.at[direction, s, t], z_next[direction]
            ).wait_recv()
            if s < 3:
                sends.append(
                    hand_on(
                        piece_a(t, a, step, *a_part(direction, s + 1)),
                        aza_ss.at[direction, s + 1, t], aza_rs.at[direction, s + 1, t], z_next[direction],
                    )
                )
            hand_on(got, aya_ss.at[t], aya_rs.at[t], other_y)
            hand_on(got, core_ss.at[t], core_rs.at[t], other_core)

    def gather_b(s, t, chain):
        for direction in (UP, DOWN):
            step = -1 - s if direction == UP else 1 + s
            got = piece_a(t, a if chain == 0 else 1 - a, step, *b_part(direction, s))
            remote(
                got, got, azb_ss.at[chain, direction, s, t], azb_rs.at[chain, direction, s, t], z_next[direction]
            ).wait_recv()
            if s < 3:
                b_hand_on(chain, direction, s + 1, t, step, *b_part(direction, s + 1))
            hand_on(got, core_ss.at[t], core_rs.at[t], other_core)

    def gather_a_end(t):
        got = acts.at[t, c, 1 - a, :, pl.ds(0, CA)]
        remote(got, got, aya_ss.at[t], aya_rs.at[t], other_y).wait_recv()
        hand_on(got, core_ss.at[t], core_rs.at[t], other_core)

    def input_gradient(t):
        side, rows = t // 2, slice(t % 2 * 128, t % 2 * 128 + 128)
        value = dot_nt(acts[0, c, side, rows, :], wgs[...]) + dot_nt(acts[1, c, side, rows, :], wus[...])
        gi[t] = value
        gi_s[t] = squared(value)

    def input_gradient_send():
        for k in range(1, NTP):
            theirs = pl.ds(pl.multiple_of(tp_off(k) * 16, 16), 16)
            copy = remote(gi_s.at[:, theirs], gi_r.at[tp], gi_ss.at[k], gi_rs.at[k], (dp, tp_off(k)))
            copy.start()
            sends.append(copy)

    def input_gradient_sum():
        mine16 = pl.ds(pl.multiple_of(tp * 16, 16), 16)
        for k in range(1, NTP):
            got = gi_r.at[tp_off(-k)]
            remote(got, got, gi_ss.at[k], gi_rs.at[k], (dp, tp_off(-k))).wait_recv()
        gi_r[tp] = jnp.zeros((OWN, 16, 512), BF16)
        for t in range(OWN):
            value = gi[t, mine16, :]
            for k in range(NTP):
                value += rooted(gi_r[k, t])
            for d in range(4):
                fin_s[pl.ds(d * 4 + t, NYZ, stride=16), :] = value[:, d * 128 : d * 128 + 128]
        for k in range(1, NYZ):
            theirs = pl.ds(pl.multiple_of(yz_off(k) * 16, 16), 16)
            copy = remote(fin_s.at[theirs], fin_r.at[yz], fin_ss.at[k], fin_rs.at[k], at(yz_off(k)))
            copy.start()
            sends.append(copy)
        fin_r[yz] = fin_s[pl.ds(pl.multiple_of(yz * 16, 16), 16), :]

    def weight_gradient(t, n):
        got = acts.at[t, 1 - c]
        remote(got, got, core_ss.at[t], core_rs.at[t], other_core).wait_recv()
        for lo, size in TILES:
            cols = slice(lo, lo + size)
            value = dot(xts[n, c], acts[t, c, :, :, cols].reshape(512, size)) + dot(
                xtp[n], acts[t, 1 - c, :, :, cols].reshape(512, size)
            )
            if t < 2:
                (og_ref, ou_ref)[t][:, cols] = value
            else:
                od_ref[cols, :] = value.T

    for t in range(2):
        gather_start(t)
    for t in range(2):
        gather_start_b(t)
    for s in range(4):
        for t in range(2):
            gather_a(s, t)
        for chain in range(2):
            for t in range(2):
                gather_b(s, t, chain)
        if s == 1:
            gather_start(2)
        if s == 2:
            gather_start_b(2)
    gather_a(0, 2)
    gather_b(0, 2, 0)
    gather_b(0, 2, 1)
    for t in range(2):
        gather_a_end(t)
    input_gradient(0)
    input_gradient(1)
    gather_a(1, 2)
    gather_b(1, 2, 0)
    gather_b(1, 2, 1)
    input_gradient(2)
    input_gradient(3)
    input_gradient_send()
    gather_a(2, 2)
    gather_b(2, 2, 0)
    gather_b(2, 2, 1)
    for n in range(2):
        remote(xtp.at[n], xtp.at[n], xt_ss.at[n], xt_rs.at[n], other_core).wait_recv()
    weight_gradient(0, 0)
    gather_a(3, 2)
    gather_b(3, 2, 0)
    gather_b(3, 2, 1)
    weight_gradient(1, 0)
    gather_a_end(2)
    input_gradient_sum()
    weight_gradient(2, 1)

    for k in range(1, NYZ):
        got = fin_r.at[yz_off(-k)]
        remote(got, got, fin_ss.at[k], fin_rs.at[k], at(yz_off(-k))).wait_recv()
    for j in range(NYZ):
        for d in range(4):
            gi_ref[:, j * 512 + d * 128 : j * 512 + d * 128 + 128] = fin_r[j, d * 4 : d * 4 + 4, :]

    for copy in sends:
        copy.wait_send()
    for t in range(3):
        sent = acts.at[t, c, a, :, pl.ds(0, CA)]
        remote(sent, sent, aya_ss.at[t], aya_rs.at[t], other_y).wait_send()
        sent = acts.at[t, c]
        remote(sent, sent, core_ss.at[t], core_rs.at[t], other_core).wait_send()


def per_device(inputs, out_grad, gate_weight, up_weight, down_weight):
    vmem = pl.BlockSpec(memory_space=pltpu.VMEM)
    hbm = pl.BlockSpec(memory_space=pl.ANY)
    dma = pltpu.SemaphoreType.DMA
    return pl.pallas_call(
        kernel,
        out_shape=(
            pltpu.VMEM((OWN, 8192), F32),
            pltpu.VMEM((DC, FF), F32),
            pltpu.VMEM((DC, FF), F32),
            pltpu.VMEM((FF, DC), F32),
        ),
        in_specs=[vmem, vmem, hbm, hbm, hbm],
        out_specs=(vmem, vmem, vmem, vmem),
        scratch_shapes=[
            pltpu.VMEM((NTP * NYZ * 16, 128), F32),
            pltpu.VMEM((2, NYZ, 16, 128), BF16),
            pltpu.VMEM((2, NTP, NYZ, 16, 128), BF16),
            pltpu.VMEM((2, 2, 512, DC), BF16),
            pltpu.VMEM((2, 2, DC, 512), BF16),
            pltpu.VMEM((2, DC, 512), BF16),
            pltpu.VMEM((2 * DC, FF), BF16),
            pltpu.VMEM((2 * DC, FF), BF16),
            pltpu.VMEM((2, FF, DC), BF16),
            pltpu.VMEM((3, 2, 256, FF), F32),
            pltpu.VMEM((3, 256, CA), BF16),
            pltpu.VMEM((3, 256, CA), BF16),
            pltpu.VMEM((2, 4, 3, 2, 32, FF - CA), BF16),
            pltpu.VMEM((2, 4, 3, 2, 32, FF - CA), BF16),
            pltpu.VMEM((2, 4, 3, 32, CA), BF16),
            pltpu.VMEM((2, 4, 3, 32, CA), BF16),
            pltpu.VMEM((3, 32, FF - CA), BF16),
            pltpu.VMEM((3, 32, FF - CA), BF16),
            pltpu.VMEM((3, 2, 2, 256, FF), BF16),
            pltpu.VMEM((OWN, 128, 512), F32),
            pltpu.VMEM((OWN, 128, 512), BF16),
            pltpu.VMEM((NTP, OWN, 16, 512), BF16),
            pltpu.VMEM((NYZ * 16, 128), F32),
            pltpu.VMEM((NYZ, 16, 128), F32),
            dma((NYZ,)), dma((NYZ,)), dma((2, NTP)), dma((2, NTP)),
            dma((3,)), dma((3,)), dma((3,)), dma((2,)), dma((2,)),
            dma((3, 8)), dma((3, 8)), dma((2, 4, 3)), dma((2, 4, 3)),
            dma((2, 4, 3)), dma((2, 4, 3)), dma((3,)), dma((3,)),
            dma((2, 4, 3)), dma((2, 4, 3)), dma((2, 2, 4, 3)), dma((2, 2, 4, 3)),
            dma((3,)), dma((3,)), dma((3,)), dma((3,)), dma((3,)), dma((3,)),
            dma((NTP,)), dma((NTP,)), dma((NYZ,)), dma((NYZ,)),
        ],
        compiler_params=pltpu.CompilerParams(
            collective_id=0, has_side_effects=True, vmem_limit_bytes=56 * 1024 * 1024
        ),
    )(inputs, out_grad, gate_weight, up_weight, down_weight)


def solution(mesh):
    in_specs = (
        P(("dp", "tp"), None),
        P(("dp", "tp"), None),
        P("dp", "tp"),
        P("dp", "tp"),
        P("tp", "dp"),
    )
    out_specs = (P(("dp", "tp"), None), P("dp", "tp"), P("dp", "tp"), P("tp", "dp"))
    return jax.shard_map(
        per_device, mesh=mesh, in_specs=in_specs, out_specs=out_specs, check_vma=False
    )
```

```python
import jax
import jax.numpy as jnp
from jax import lax
from jax.experimental import pallas as pl
from jax.experimental.pallas import tpu as pltpu
from jax.sharding import PartitionSpec as P

MESH = pl.DeviceIdType.MESH
F32, BF16 = jnp.float32, jnp.bfloat16
NZ, NYZ, NTP = 8, 16, 8
OWN = 4
DC = 256
FF = 1920
CA = 896
HA = 512
HB = 512
UP, DOWN = 0, 1
TILES = ((0, 512), (512, 384), (896, 512), (1408, 512))
FAR_FIRST = (4, 3, -3, 2, -2, 1, -1, 0)


SCALE = 2.0**19
TINY = 2.0**-126


def coded(v):
    return (v * jnp.abs(v) * (v * v)).astype(BF16)


def decoded(y):
    y = y.astype(F32)
    r = lax.rsqrt(jnp.maximum(jnp.abs(y), TINY))
    return y * r * r * lax.rsqrt(r)


def squared(v):
    return (v * jnp.abs(v)).astype(BF16)


def rooted(y):
    y = y.astype(F32)
    return y * lax.rsqrt(jnp.maximum(jnp.abs(y), TINY))


def dot(a, b):
    return jnp.dot(a, b, preferred_element_type=F32)


def dot_nt(a, b):
    return lax.dot_general(a, b, (((1,), (1,)), ((), ())), preferred_element_type=F32)


def kernel(
    x_ref, g_ref, wg_ref, wu_ref, wd_ref,
    gi_ref, og_ref, ou_ref, od_ref,
    stage, first, tokens, xs, xts, xtp, wgs, wus, wds, part,
    ya_s, ya_r, zb_s, zb_r, za_s, za_r, yb_s, yb_r, acts,
    gi, gi_s, gi_r, fin_s, fin_r,
    first_ss, first_rs, tok_ss, tok_rs, w_ls, w_ss, w_rs, xt_ss, xt_rs,
    ya_ss, ya_rs, zb_ss, zb_rs, za_ss, za_rs, yb_ss, yb_rs,
    aza_ss, aza_rs, azb_ss, azb_rs, aya_ss, aya_rs, ayb_ss, ayb_rs, core_ss, core_rs,
    gi_ss, gi_rs, fin_ss, fin_rs,
):
    dp, tp = lax.axis_index("dp"), lax.axis_index("tp")
    c = lax.rem(dp, 2)
    yz = lax.div(dp, 2)
    z = lax.rem(yz, NZ)
    a = lax.div(yz, NZ)

    def at(yz_to):
        return (yz_to * 2 + c, tp)

    def at_z(step):
        return at(a * NZ + lax.rem(z + step + NZ, NZ))

    other_y = at((1 - a) * NZ + z)
    other_core = (yz * 2 + 1 - c, tp)
    z_next = (at_z(1), at_z(-1))

    def yz_off(k):
        return lax.rem(yz + k + NYZ, NYZ)

    def tp_off(k):
        return lax.rem(tp + k + NTP, NTP)

    def remote(src, dst, ss, rs, to):
        return pltpu.make_async_remote_copy(
            src_ref=src, dst_ref=dst, send_sem=ss, recv_sem=rs, device_id=to, device_id_type=MESH
        )

    def z_rows(step):
        return pl.ds(pl.multiple_of(lax.rem(z + step + NZ, NZ) * 32, 32), 32)

    barrier = pltpu.get_barrier_semaphore()
    for k in range(1, NYZ):
        pl.semaphore_signal(barrier, inc=1, device_id=at(yz_off(k)), device_id_type=MESH)
    for k in range(1, NTP):
        pl.semaphore_signal(barrier, inc=1, device_id=(dp, tp_off(k)), device_id_type=MESH)
    pl.semaphore_signal(barrier, inc=1, device_id=other_core, device_id_type=MESH)

    w_local = []
    mine = pl.ds(pl.multiple_of(c * DC, DC), DC)
    slots = (wgs.at[mine], wus.at[mine], wds.at[c])
    for i, (src, dst) in enumerate(zip((wg_ref, wu_ref, wd_ref), slots)):
        copy = pltpu.make_async_copy(src, dst, w_ls.at[i])
        copy.start()
        w_local.append(copy)

    for n, ref in enumerate((x_ref, g_ref)):
        whole = ref[...].astype(F32)
        for i in range(64):
            stage[i * 4 : i * 4 + 4, :] = whole[:, i * 128 : i * 128 + 128]
        first[n] = stage[0:256, :].astype(BF16).reshape(NYZ, 16, 128)

    pl.semaphore_wait(barrier, NYZ - 1 + NTP - 1 + 1)

    sends = []
    for k in range(1, NYZ):
        copy = remote(
            first.at[:, yz_off(k)], tokens.at[:, tp, yz], first_ss.at[k], first_rs.at[k], at(yz_off(k))
        )
        copy.start()
        sends.append(copy)
    for i, (src, dst) in enumerate(zip((wg_ref, wu_ref, wd_ref), slots)):
        copy = remote(src, dst, w_ss.at[i], w_rs.at[i], other_core)
        copy.start()
        sends.append(copy)
    tokens[:, tp, yz] = first[:, yz]
    for k in range(1, NYZ):
        piece = tokens.at[:, tp, yz_off(-k)]
        remote(piece, piece, first_ss.at[k], first_rs.at[k], at(yz_off(-k))).wait_recv()
    def tokens_start(n):
        for k in range(1, NTP):
            copy = remote(
                tokens.at[n, tp], tokens.at[n, tp], tok_ss.at[n, k], tok_rs.at[n, k], (dp, tp_off(k))
            )
            copy.start()
            sends.append(copy)

    def tokens_wait(n):
        for k in range(1, NTP):
            piece = tokens.at[n, tp_off(-k)]
            remote(piece, piece, tok_ss.at[n, k], tok_rs.at[n, k], (dp, tp_off(-k))).wait_recv()

    def tokens_end(n):
        stage[...] = tokens[n].reshape(NTP * NYZ * 16, 128).astype(F32)
        for d in range(4):
            for t in range(OWN):
                block = stage[pl.ds(d * 4 + t, 128, stride=16), :]
                rows, cols = slice(t * 128, t * 128 + 128), slice(d % 2 * 128, d % 2 * 128 + 128)
                xs[n, d // 2, rows, cols] = block.astype(BF16)

    def transpose_tokens(n):
        for h in range(2):
            xts[n, h] = xs[n, h].astype(F32).T.astype(BF16)
        copy = remote(xts.at[n, 1 - c], xtp.at[n], xt_ss.at[n], xt_rs.at[n], other_core)
        copy.start()
        sends.append(copy)

    def take_weight(i):
        w_local[i].wait()
        theirs = (
            wgs.at[pl.ds(pl.multiple_of((1 - c) * DC, DC), DC)],
            wus.at[pl.ds(pl.multiple_of((1 - c) * DC, DC), DC)],
            wds.at[1 - c],
        )[i]
        remote(theirs, theirs, w_ss.at[i], w_rs.at[i], other_core).wait_recv()

    def b_cols(direction, s):
        if s == 0:
            return (CA, CA + HB) if direction == UP else (CA + HB, FF)
        return (CA, FF)

    def a_cols(direction, s):
        if s == 0:
            return (0, HA) if direction == UP else (HA, CA)
        return (0, CA)

    def first_products(t):
        if t < 2:
            w = (wgs, wus)[t]
            for lo, size in TILES:
                cols = slice(lo, lo + size)
                value = dot(xs[0, 0], w[0:DC, cols]) + dot(xs[0, 1], w[DC : 2 * DC, cols])
                part[t, :, :, cols] = (value * SCALE).reshape(2, 256, size)
        else:
            for lo, size in TILES:
                cols = slice(lo, lo + size)
                value = dot_nt(xs[1, 0], wds[0, cols, :]) + dot_nt(xs[1, 1], wds[1, cols, :])
                part[t, :, :, cols] = (value * SCALE).reshape(2, 256, size)

    def y_send(t):
        ya_s[t] = coded(part[t, 1 - a, :, 0:CA])
        for i, rows in enumerate(y_pieces(t)):
            copy = remote(ya_s.at[t, rows], ya_r.at[t, rows], ya_ss.at[t, i], ya_rs.at[t, i], other_y)
            copy.start()
            sends.append(copy)

    def y_pieces(t):
        return [slice(0, 256)] if t < 2 else [z_rows(step) for step in FAR_FIRST]

    def y_take(t, i):
        rows = y_pieces(t)[i]
        remote(ya_r.at[t, rows], ya_r.at[t, rows], ya_ss.at[t, i], ya_rs.at[t, i], other_y).wait_recv()
        part[t, a, rows, 0:CA] = part[t, a, rows, 0:CA] + decoded(ya_r[t, rows, :])

    def b_message(buf, direction, s, t):
        lo, hi = b_cols(direction, s)
        return buf.at[direction, s, t, :, :, pl.ds(lo - CA, hi - lo)]

    def a_message(buf, direction, s, t):
        lo, hi = a_cols(direction, s)
        return buf.at[direction, s, t, :, pl.ds(lo, hi - lo)]

    def b_wait(direction, s, t):
        got = b_message(zb_r, direction, s, t)
        remote(got, got, zb_ss.at[direction, s, t], zb_rs.at[direction, s, t], z_next[direction]).wait_recv()

    def a_wait(direction, s, t):
        got = a_message(za_r, direction, s, t)
        remote(got, got, za_ss.at[direction, s, t], za_rs.at[direction, s, t], z_next[direction]).wait_recv()

    def b_step(s, t):
        for direction in (UP, DOWN):
            rows = z_rows(4 - s if direction == UP else s - 4)
            lo, hi = b_cols(direction, s)
            if s == 0:
                zb_s[direction, s, t, :, :, lo - CA : hi - CA] = coded(part[t, :, rows, lo:hi])
            else:
                b_wait(direction, s - 1, t)
                glo, ghi = b_cols(direction, s - 1)
                zb_s[direction, s, t, :, :, glo - CA : ghi - CA] = coded(
                    part[t, :, rows, glo:ghi]
                    + decoded(zb_r[direction, s - 1, t, :, :, glo - CA : ghi - CA])
                )
                if s == 1:
                    nlo, nhi = b_cols(1 - direction, 0)
                    zb_s[direction, s, t, :, :, nlo - CA : nhi - CA] = coded(part[t, :, rows, nlo:nhi])
            copy = remote(
                b_message(zb_s, direction, s, t), b_message(zb_r, direction, s, t),
                zb_ss.at[direction, s, t], zb_rs.at[direction, s, t], z_next[direction],
            )
            copy.start()
            sends.append(copy)

    def b_end(t):
        own = z_rows(0)
        for direction in (UP, DOWN):
            b_wait(direction, 3, t)
        total = part[t, :, own, CA:FF] + decoded(zb_r[UP, 3, t]) + decoded(zb_r[DOWN, 3, t])
        part[t, :, own, CA:FF] = total
        yb_s[t] = coded(part[t, 1 - a, own, CA:FF])
        copy = remote(yb_s.at[t], yb_r.at[t], yb_ss.at[t], yb_rs.at[t], other_y)
        copy.start()
        sends.append(copy)

    def a_start(t):
        y_take(t, 0)
        a_step(0, t)

    def a_step(s, t):
        if t == 2 and s > 0:
            y_take(t, 2 * s - 1)
            y_take(t, 2 * s)
        for direction in (UP, DOWN):
            rows = z_rows(4 - s if direction == UP else s - 4)
            lo, hi = a_cols(direction, s)
            if s == 0:
                za_s[direction, s, t, :, lo:hi] = coded(part[t, a, rows, lo:hi])
            else:
                a_wait(direction, s - 1, t)
                glo, ghi = a_cols(direction, s - 1)
                za_s[direction, s, t, :, glo:ghi] = coded(
                    part[t, a, rows, glo:ghi] + decoded(za_r[direction, s - 1, t, :, glo:ghi])
                )
                if s == 1:
                    nlo, nhi = a_cols(1 - direction, 0)
                    za_s[direction, s, t, :, nlo:nhi] = coded(part[t, a, rows, nlo:nhi])
            copy = remote(
                a_message(za_s, direction, s, t), a_message(za_r, direction, s, t),
                za_ss.at[direction, s, t], za_rs.at[direction, s, t], z_next[direction],
            )
            copy.start()
            sends.append(copy)

    tokens_start(0)
    tokens_wait(0)
    tokens_start(1)
    tokens_end(0)
    take_weight(0)
    first_products(0)
    b_step(0, 0)
    y_send(0)
    take_weight(1)
    first_products(1)
    b_step(0, 1)
    y_send(1)
    b_step(1, 0)
    b_step(1, 1)
    tokens_wait(1)
    tokens_end(1)
    take_weight(2)
    first_products(2)
    b_step(0, 2)
    y_send(2)
    b_step(2, 0)
    b_step(2, 1)
    b_step(1, 2)
    transpose_tokens(0)
    transpose_tokens(1)
    a_start(0)
    b_step(3, 0)
    b_step(3, 1)
    b_step(2, 2)
    a_start(1)
    a_step(1, 0)
    b_end(0)
    b_end(1)
    b_step(3, 2)
    a_start(2)
    a_step(1, 1)
    a_step(2, 0)
    b_end(2)
    a_step(1, 2)
    a_step(2, 1)
    a_step(3, 0)
    a_step(2, 2)
    a_step(3, 1)
    a_step(3, 2)

    own = z_rows(0)
    y_take(2, 7)
    for t in range(3):
        for direction in (UP, DOWN):
            a_wait(direction, 3, t)
        remote(yb_r.at[t], yb_r.at[t], yb_ss.at[t], yb_rs.at[t], other_y).wait_recv()

    def total(t, lo, hi):
        if hi <= CA:
            value = (
                part[t, a, own, lo:hi]
                + decoded(za_r[UP, 3, t, :, lo:hi])
                + decoded(za_r[DOWN, 3, t, :, lo:hi])
            )
        else:
            value = part[t, a, own, lo:hi] + decoded(yb_r[t, :, lo - CA : hi - CA])
        return value * (1.0 / SCALE)

    for lo, size in TILES:
        hi = lo + size
        gate, up, back = total(0, lo, hi), total(1, lo, hi), total(2, lo, hi)
        s = jax.nn.sigmoid(gate)
        silu = gate * s
        acts[0, c, a, own, lo:hi] = (back * up * s * (1.0 + gate * (1.0 - s))).astype(BF16)
        acts[1, c, a, own, lo:hi] = (back * silu).astype(BF16)
        acts[2, c, a, own, lo:hi] = (silu * up).astype(BF16)

    def hand_on(region, ss, rs, to):
        copy = remote(region, region, ss, rs, to)
        copy.start()
        return copy

    def piece_a(t, side, step, lo=0, hi=CA):
        return acts.at[t, c, side, z_rows(step), pl.ds(lo, hi - lo)]


    def a_part(direction, s):
        return (0, CA) if s < 3 else ((0, HA) if direction == UP else (HA, CA))

    def b_part(direction, s):
        return (CA, FF) if s < 3 else ((CA, CA + HB) if direction == UP else (CA + HB, FF))

    def gather_start(t):
        sends.append(
            hand_on(acts.at[t, c, a, own, pl.ds(CA, FF - CA)], ayb_ss.at[t], ayb_rs.at[t], other_y)
        )
        for direction in (UP, DOWN):
            sends.append(
                hand_on(piece_a(t, a, 0), aza_ss.at[direction, 0, t], aza_rs.at[direction, 0, t], z_next[direction])
            )
        hand_on(piece_a(t, a, 0), aya_ss.at[t], aya_rs.at[t], other_y)
        hand_on(acts.at[t, c, a, own], core_ss.at[t], core_rs.at[t], other_core)
        for direction in (UP, DOWN):
            b_hand_on(0, direction, 0, t, 0, CA, FF)

    def b_hand_on(chain, direction, s, t, step, lo, hi):
        sends.append(
            hand_on(
                piece_a(t, a if chain == 0 else 1 - a, step, lo, hi),
                azb_ss.at[chain, direction, s, t], azb_rs.at[chain, direction, s, t], z_next[direction],
            )
        )

    def gather_start_b(t):
        theirs = acts.at[t, c, 1 - a, own, pl.ds(CA, FF - CA)]
        remote(theirs, theirs, ayb_ss.at[t], ayb_rs.at[t], other_y).wait_recv()
        for direction in (UP, DOWN):
            b_hand_on(1, direction, 0, t, 0, CA, FF)
        hand_on(theirs, core_ss.at[t], core_rs.at[t], other_core)

    def gather_a(s, t):
        for direction in (UP, DOWN):
            step = -1 - s if direction == UP else 1 + s
            got = piece_a(t, a, step, *a_part(direction, s))
            remote(
                got, got, aza_ss.at[direction, s, t], aza_rs.at[direction, s, t], z_next[direction]
            ).wait_recv()
            if s < 3:
                sends.append(
                    hand_on(
                        piece_a(t, a, step, *a_part(direction, s + 1)),
                        aza_ss.at[direction, s + 1, t], aza_rs.at[direction, s + 1, t], z_next[direction],
                    )
                )
            hand_on(got, aya_ss.at[t], aya_rs.at[t], other_y)
            hand_on(got, core_ss.at[t], core_rs.at[t], other_core)

    def gather_b(s, t, chain):
        for direction in (UP, DOWN):
            step = -1 - s if direction == UP else 1 + s
            got = piece_a(t, a if chain == 0 else 1 - a, step, *b_part(direction, s))
            remote(
                got, got, azb_ss.at[chain, direction, s, t], azb_rs.at[chain, direction, s, t], z_next[direction]
            ).wait_recv()
            if s < 3:
                b_hand_on(chain, direction, s + 1, t, step, *b_part(direction, s + 1))
            hand_on(got, core_ss.at[t], core_rs.at[t], other_core)

    def gather_a_end(t):
        got = acts.at[t, c, 1 - a, :, pl.ds(0, CA)]
        remote(got, got, aya_ss.at[t], aya_rs.at[t], other_y).wait_recv()
        hand_on(got, core_ss.at[t], core_rs.at[t], other_core)

    def input_gradient(side, i):
        t, rows = side * 2 + i, slice(i * 128, i * 128 + 128)
        value = dot_nt(acts[0, c, side, rows, :], wgs[...]) + dot_nt(acts[1, c, side, rows, :], wus[...])
        gi[t] = value
        gi_s[t] = squared(value)

    def input_gradient_send():
        for k in range(1, NTP):
            theirs = pl.ds(pl.multiple_of(tp_off(k) * 16, 16), 16)
            copy = remote(gi_s.at[:, theirs], gi_r.at[tp], gi_ss.at[k], gi_rs.at[k], (dp, tp_off(k)))
            copy.start()
            sends.append(copy)

    def input_gradient_sum():
        mine16 = pl.ds(pl.multiple_of(tp * 16, 16), 16)
        for k in range(1, NTP):
            got = gi_r.at[tp_off(-k)]
            remote(got, got, gi_ss.at[k], gi_rs.at[k], (dp, tp_off(-k))).wait_recv()
        gi_r[tp] = jnp.zeros((OWN, 16, 512), BF16)
        for t in range(OWN):
            value = gi[t, mine16, :]
            for k in range(NTP):
                value += rooted(gi_r[k, t])
            for d in range(4):
                fin_s[pl.ds(d * 4 + t, NYZ, stride=16), :] = value[:, d * 128 : d * 128 + 128]
        for k in range(1, NYZ):
            theirs = pl.ds(pl.multiple_of(yz_off(k) * 16, 16), 16)
            copy = remote(fin_s.at[theirs], fin_r.at[yz], fin_ss.at[k], fin_rs.at[k], at(yz_off(k)))
            copy.start()
            sends.append(copy)
        fin_r[yz] = fin_s[pl.ds(pl.multiple_of(yz * 16, 16), 16), :]

    def weight_gradient(t, n):
        got = acts.at[t, 1 - c]
        remote(got, got, core_ss.at[t], core_rs.at[t], other_core).wait_recv()
        for lo, size in TILES:
            cols = slice(lo, lo + size)
            value = dot(xts[n, c], acts[t, c, :, :, cols].reshape(512, size)) + dot(
                xtp[n], acts[t, 1 - c, :, :, cols].reshape(512, size)
            )
            if t < 2:
                (og_ref, ou_ref)[t][:, cols] = value
            else:
                od_ref[cols, :] = value.T

    for t in range(2):
        gather_start(t)
    for t in range(2):
        gather_start_b(t)
    for s in range(4):
        for t in range(2):
            gather_a(s, t)
        for chain in range(2):
            for t in range(2):
                gather_b(s, t, chain)
        if s == 1:
            gather_start(2)
        if s == 2:
            gather_start_b(2)
    gather_a(0, 2)
    gather_b(0, 2, 0)
    gather_b(0, 2, 1)
    input_gradient(a, 0)
    for t in range(2):
        gather_a_end(t)
    input_gradient(a, 1)
    gather_a(1, 2)
    gather_b(1, 2, 0)
    gather_b(1, 2, 1)
    input_gradient(1 - a, 0)
    input_gradient(1 - a, 1)
    input_gradient_send()
    gather_a(2, 2)
    gather_b(2, 2, 0)
    gather_b(2, 2, 1)
    for n in range(2):
        remote(xtp.at[n], xtp.at[n], xt_ss.at[n], xt_rs.at[n], other_core).wait_recv()
    weight_gradient(0, 0)
    gather_a(3, 2)
    gather_b(3, 2, 0)
    gather_b(3, 2, 1)
    weight_gradient(1, 0)
    input_gradient_sum()
    gather_a_end(2)
    weight_gradient(2, 1)

    for k in range(1, NYZ):
        got = fin_r.at[yz_off(-k)]
        remote(got, got, fin_ss.at[k], fin_rs.at[k], at(yz_off(-k))).wait_recv()
    for j in range(NYZ):
        for d in range(4):
            gi_ref[:, j * 512 + d * 128 : j * 512 + d * 128 + 128] = fin_r[j, d * 4 : d * 4 + 4, :]

    for copy in sends:
        copy.wait_send()
    for t in range(3):
        sent = acts.at[t, c, a, :, pl.ds(0, CA)]
        remote(sent, sent, aya_ss.at[t], aya_rs.at[t], other_y).wait_send()
        sent = acts.at[t, c]
        remote(sent, sent, core_ss.at[t], core_rs.at[t], other_core).wait_send()


def per_device(inputs, out_grad, gate_weight, up_weight, down_weight):
    vmem = pl.BlockSpec(memory_space=pltpu.VMEM)
    hbm = pl.BlockSpec(memory_space=pl.ANY)
    dma = pltpu.SemaphoreType.DMA
    return pl.pallas_call(
        kernel,
        out_shape=(
            pltpu.VMEM((OWN, 8192), F32),
            pltpu.VMEM((DC, FF), F32),
            pltpu.VMEM((DC, FF), F32),
            pltpu.VMEM((FF, DC), F32),
        ),
        in_specs=[vmem, vmem, hbm, hbm, hbm],
        out_specs=(vmem, vmem, vmem, vmem),
        scratch_shapes=[
            pltpu.VMEM((NTP * NYZ * 16, 128), F32),
            pltpu.VMEM((2, NYZ, 16, 128), BF16),
            pltpu.VMEM((2, NTP, NYZ, 16, 128), BF16),
            pltpu.VMEM((2, 2, 512, DC), BF16),
            pltpu.VMEM((2, 2, DC, 512), BF16),
            pltpu.VMEM((2, DC, 512), BF16),
            pltpu.VMEM((2 * DC, FF), BF16),
            pltpu.VMEM((2 * DC, FF), BF16),
            pltpu.VMEM((2, FF, DC), BF16),
            pltpu.VMEM((3, 2, 256, FF), F32),
            pltpu.VMEM((3, 256, CA), BF16),
            pltpu.VMEM((3, 256, CA), BF16),
            pltpu.VMEM((2, 4, 3, 2, 32, FF - CA), BF16),
            pltpu.VMEM((2, 4, 3, 2, 32, FF - CA), BF16),
            pltpu.VMEM((2, 4, 3, 32, CA), BF16),
            pltpu.VMEM((2, 4, 3, 32, CA), BF16),
            pltpu.VMEM((3, 32, FF - CA), BF16),
            pltpu.VMEM((3, 32, FF - CA), BF16),
            pltpu.VMEM((3, 2, 2, 256, FF), BF16),
            pltpu.VMEM((OWN, 128, 512), F32),
            pltpu.VMEM((OWN, 128, 512), BF16),
            pltpu.VMEM((NTP, OWN, 16, 512), BF16),
            pltpu.VMEM((NYZ * 16, 128), F32),
            pltpu.VMEM((NYZ, 16, 128), F32),
            dma((NYZ,)), dma((NYZ,)), dma((2, NTP)), dma((2, NTP)),
            dma((3,)), dma((3,)), dma((3,)), dma((2,)), dma((2,)),
            dma((3, 8)), dma((3, 8)), dma((2, 4, 3)), dma((2, 4, 3)),
            dma((2, 4, 3)), dma((2, 4, 3)), dma((3,)), dma((3,)),
            dma((2, 4, 3)), dma((2, 4, 3)), dma((2, 2, 4, 3)), dma((2, 2, 4, 3)),
            dma((3,)), dma((3,)), dma((3,)), dma((3,)), dma((3,)), dma((3,)),
            dma((NTP,)), dma((NTP,)), dma((NYZ,)), dma((NYZ,)),
        ],
        compiler_params=pltpu.CompilerParams(
            collective_id=0, has_side_effects=True, vmem_limit_bytes=56 * 1024 * 1024
        ),
    )(inputs, out_grad, gate_weight, up_weight, down_weight)


def solution(mesh):
    in_specs = (
        P(("dp", "tp"), None),
        P(("dp", "tp"), None),
        P("dp", "tp"),
        P("dp", "tp"),
        P("tp", "dp"),
    )
    out_specs = (P(("dp", "tp"), None), P("dp", "tp"), P("dp", "tp"), P("tp", "dp"))
    return jax.shard_map(
        per_device, mesh=mesh, in_specs=in_specs, out_specs=out_specs, check_vma=False
    )
```
